32 devices in a mesh: outer: 4 (over z), inner: 8 (over y, x, core).
Axes of the slice: x: 2, y: 2, z: 4, core: 2. Of those that a mesh axis runs over, the one named last changes fastest.
Arguments:
- context: bfloat16 [4096, 4096], P(('outer', 'inner')), may hold values from -5 to 5
- query_acts: bfloat16 [64, 4096], replicated, may hold values from -5 to 5
- norm_gain: float32 [4096], replicated, may hold values from 0.25 to 1.75
- w_query: bfloat16 [4096, 2048], P('inner'), may hold values from -0.078125 to 0.078125
- w_key: bfloat16 [4096, 512], P('inner'), may hold values from -0.453125 to 0.453125
- value_weight: bfloat16 [4096, 512], P('inner'), may hold values from -0.09375 to 0.09375
- lengths: int32 [32], replicated, may hold values from 64 to 128, as said below
Outputs:
- block_out: bfloat16 [4096, 2048], P(('outer', 'inner'))
- query_out: bfloat16 [64, 2048], replicated
The draws below stay inside these ranges and needn't reach their ends.
Inputs may be any that keep to these rules, and one draw needn't show every extreme that they name: `lengths`: valid tokens of a block are its first ones; the rest of it is padding.
All inputs are finite; a program needn't handle non-finite values.
Results may differ from the reference program's by a relative error of at most 0.004.
The reference program's roundings to bfloat16 on the way count: a program that leaves them out, or rounds other values in their place, can miss the bound.
Values may be sent and summed in bfloat16 or wider, within the bound.
A program may use at most 320 MiB of HBM per device.

```python
import jax
import jax.numpy as jnp
from jax import lax

MODEL_WIDTH = 4096
QUERY_HEADS = 16
KEY_VALUE_HEADS = 4
HEAD_SIZE = 128
BLK = 128
QTOK = 64
TOKENS = 4096


def coarse_rows(stream, extent):
    return jnp.clip(jax.random.normal(stream, extent, jnp.float32), -5.0, 5.0)


def query_probs(key):
    return coarse_rows(jax.random.fold_in(key, 17), (MODEL_WIDTH, QUERY_HEADS * HEAD_SIZE)) * MODEL_WIDTH ** (-0.5)


def draw_context(key, part):
    drawn = coarse_rows(jax.random.fold_in(key, 11), (TOKENS, MODEL_WIDTH))
    return drawn.astype(jnp.bfloat16)


def draw_query_acts(key, part):
    drawn = coarse_rows(jax.random.fold_in(key, 13), (QTOK, MODEL_WIDTH))
    return drawn.astype(jnp.bfloat16)


def draw_w_query(key, part):
    return query_probs(key).astype(jnp.bfloat16)


def draw_w_key(key, part):
    small_noise = coarse_rows(jax.random.fold_in(key, 23), (MODEL_WIDTH, KEY_VALUE_HEADS * HEAD_SIZE)) * MODEL_WIDTH ** (-0.5)
    return small_noise.astype(jnp.bfloat16)


def draw_lengths(key, part):
    blocks = TOKENS // BLK
    drawn = jax.random.randint(jax.random.fold_in(key, 41), (blocks,), BLK // 2, BLK + 1, dtype=jnp.int32)
    longest = jax.random.randint(jax.random.fold_in(key, 42), (), 0, blocks, dtype=jnp.int32)
    shortest = (longest + 1 + jax.random.randint(jax.random.fold_in(key, 43), (), 0, blocks - 1, dtype=jnp.int32)) % blocks
    places = jnp.arange(blocks, dtype=jnp.int32)
    drawn = jnp.where(places == longest, BLK, drawn)
    return jnp.where(places == shortest, BLK // 2, drawn).astype(jnp.int32)


def block_scale(stream_key, dims, shards, least, high):
    def one(dim, shards_of):
        draws = jax.random.uniform(jax.random.fold_in(jax.random.fold_in(stream_key, 6), dim), (shards_of,), jnp.float32, least / len(shards), high / len(shards))
        return jnp.repeat(jnp.exp(draws), dims[dim] // shards_of).reshape((-1,) + (1,) * (len(dims) - dim - 1))

    factor_of = one(*shards[0])
    for cut in shards[1:]:
        factor_of = factor_of * one(*cut)
    return factor_of


def centred(key, shape, deviation, limit, cuts=(), kind=jnp.bfloat16):
    factor_of = block_scale(key, shape, cuts, -0.22, 0.18) if cuts else 1.0
    array = jax.random.normal(key, shape, jnp.float32) * deviation * factor_of
    return jnp.minimum(jnp.maximum(array, -limit), limit).astype(kind)


def setup_inputs(seed: int = 0) -> dict:
    key_list = jax.random.split(jax.random.key(seed), 8)
    return {
        "context": draw_context(jax.random.fold_in(key_list[7], 71), 0),
        "query_acts": draw_query_acts(jax.random.fold_in(key_list[7], 71), 0),
        "norm_gain": jnp.clip(1.0 + 0.15 * jax.random.normal(key_list[2], (MODEL_WIDTH,), jnp.float32), 0.25, 1.75),
        "w_query": draw_w_query(jax.random.fold_in(key_list[7], 71), 0),
        "w_key": draw_w_key(jax.random.fold_in(key_list[7], 71), 0),
        "value_weight": centred(key_list[5], (MODEL_WIDTH, KEY_VALUE_HEADS * HEAD_SIZE), MODEL_WIDTH ** -0.5, 0.09375, ((0, 8),)),
        "lengths": draw_lengths(jax.random.fold_in(key_list[7], 71), 0),
    }


epsilon = 1e-05

def normalize(matrix, norm_gain):
    widened = matrix.astype(jnp.float32)
    factor = lax.rsqrt(lax.optimization_barrier(jnp.mean(widened * widened, axis=-1, keepdims=True)) + epsilon)
    return (widened * factor * norm_gain).astype(jnp.bfloat16)

def project(normed, weight):
    return jnp.dot(normed, weight, preferred_element_type=jnp.float32).astype(jnp.bfloat16)

def widen_rounded(value_matrix):
    return lax.optimization_barrier(value_matrix.astype(jnp.bfloat16)).astype(jnp.float32)

def attend_part(query_rows, key_row_block, value_matrix, allowed):
    count_of_rows = query_rows.shape[0]
    head_groups = query_rows.reshape(count_of_rows, KEY_VALUE_HEADS, QUERY_HEADS // KEY_VALUE_HEADS, HEAD_SIZE).astype(jnp.float32)
    per_head_keys = key_row_block.reshape(key_row_block.shape[0], KEY_VALUE_HEADS, HEAD_SIZE).astype(jnp.float32)
    per_head_values = value_matrix.reshape(value_matrix.shape[0], KEY_VALUE_HEADS, HEAD_SIZE).astype(jnp.float32)
    scores = jnp.einsum('rhgd,khd->hgrk', head_groups, per_head_keys) * HEAD_SIZE ** (-0.5)
    scores = jnp.where(allowed, scores, -jnp.inf)
    maxima = lax.optimization_barrier(jnp.max(scores, axis=-1))
    weights = jnp.exp(scores - maxima[..., None])
    sum_exp = lax.optimization_barrier(jnp.sum(weights, axis=-1))
    numerator = jnp.einsum('hgrk,khd->rhgd', widen_rounded(weights), per_head_values)
    return (maxima.reshape(QUERY_HEADS, count_of_rows), sum_exp.reshape(QUERY_HEADS, count_of_rows), numerator.reshape(count_of_rows, QUERY_HEADS * HEAD_SIZE))

def spread(factor):
    return jnp.repeat(factor.T, HEAD_SIZE, axis=1)

def combine(former, latter):
    maxima = jnp.maximum(former[0], latter[0])
    scale_one = jnp.exp(former[0] - maxima)
    scale_two = jnp.exp(latter[0] - maxima)
    return (maxima, former[1] * scale_one + latter[1] * scale_two, former[2] * spread(scale_one) + latter[2] * spread(scale_two))

def finish(pieces):
    return (pieces[2] / spread(pieces[1])).astype(jnp.bfloat16)

def reference(context, query_acts, norm_gain, w_query, w_key, value_weight, lengths):
    block_count = lengths.shape[0]
    anchor_normed = normalize(context[:BLK], norm_gain)
    anchor_keys = project(anchor_normed, w_key)
    anchor_values = project(anchor_normed, value_weight)
    anchor_length = lengths[0]
    query_normed = normalize(query_acts, norm_gain)
    query_q = project(query_normed, w_query)
    query_k = project(query_normed, w_key)
    query_v = project(query_normed, value_weight)
    places = jnp.arange(BLK, dtype=jnp.int32)
    causal = places[:, None] >= places[None, :]

    def one_block(running, inputs):
        matrix, length, block_index = inputs
        normed = normalize(matrix, norm_gain)
        block_q = project(normed, w_query)
        block_k = project(normed, w_key)
        block_v = project(normed, value_weight)
        own_allowed = causal & (places[None, :] < length)
        anchor_allowed = jnp.broadcast_to((places[None, :] < anchor_length) & (block_index > 0), (BLK, BLK))
        allowed = jnp.concatenate([anchor_allowed, own_allowed], axis=1)
        key_row_block = jnp.concatenate([anchor_keys, block_k], axis=0)
        value_rows = jnp.concatenate([anchor_values, block_v], axis=0)
        outputs = finish(attend_part(block_q, key_row_block, value_rows, allowed))
        reached = jnp.broadcast_to(places[None, :] < length, (QTOK, BLK))
        running = combine(running, attend_part(query_q, block_k, block_v, reached))
        return (running, outputs)
    initial = (jnp.full((QUERY_HEADS, QTOK), -jnp.inf, jnp.float32), jnp.zeros((QUERY_HEADS, QTOK), jnp.float32), jnp.zeros((QTOK, QUERY_HEADS * HEAD_SIZE), jnp.float32))
    running, outputs = lax.scan(one_block, initial, (context.reshape(block_count, BLK, MODEL_WIDTH), lengths, jnp.arange(block_count, dtype=jnp.int32)))
    query_places = jnp.arange(QTOK, dtype=jnp.int32)
    self_part = attend_part(query_q, query_k, query_v, query_places[:, None] >= query_places[None, :])
    query_out = finish(combine(running, self_part))
    return (outputs.reshape(block_count * BLK, QUERY_HEADS * HEAD_SIZE), query_out)
```

```python
import jax
import jax.numpy as jnp
from jax import lax
from jax.experimental import pallas as pl
from jax.experimental.pallas import tpu as pltpu
from jax.sharding import PartitionSpec as P

QUERY_HEADS = 16
KEY_VALUE_HEADS = 4
HEAD_SIZE = 128


epsilon = 1e-05


def broadcast(block, axis, owner):
    block = jnp.where(lax.axis_index(axis) == owner, block, jnp.zeros_like(block))
    return lax.psum(block, axis)


def normalize(matrix, norm_gain):
    widened = matrix.astype(jnp.float32)
    factor = lax.rsqrt(jnp.mean(widened * widened, axis=-1, keepdims=True) + epsilon)
    return (widened * factor * norm_gain).astype(jnp.bfloat16)


def chip_peer(chip, step):
    offset = (step + 1) % 4
    return (chip // 2 + offset // 2) % 2 * 2 + (chip + offset) % 2


def normalize_rows(source, gain, first, count):
    widened = source[pl.ds(first, count), :].astype(jnp.float32)
    factor = lax.rsqrt(jnp.mean(widened * widened, axis=-1, keepdims=True) + epsilon)
    return (widened * factor * gain[...]).astype(jnp.bfloat16)


def projection_kernel(
    context, query_acts, gain, w_query, w_key, value_weight, context_out, query_out,
    twin_query, twin_key, twin_value, sliced, query_sliced, gathered, partial, arrived,
    own_query, peer_query, twin_send, twin_recv, row_send, row_recv, sum_send, sum_recv,
    query_send, query_recv,
):
    inner = lax.axis_index("inner")
    chip, core = inner // 2, inner % 2
    twin = chip * 2 + 1 - core

    def peer(step):
        return chip_peer(chip, step)

    def remote(source, target, send, recv, device):
        return pltpu.make_async_remote_copy(
            src_ref=source, dst_ref=target, send_sem=send, recv_sem=recv,
            device_id={"inner": device}, device_id_type=pl.DeviceIdType.MESH,
        )

    barrier = pltpu.get_barrier_semaphore()
    pl.semaphore_signal(barrier, inc=1, device_id={"inner": twin}, device_id_type=pl.DeviceIdType.MESH)
    for step in range(3):
        pl.semaphore_signal(
            barrier, inc=1, device_id={"inner": peer(step) * 2 + core},
            device_id_type=pl.DeviceIdType.MESH,
        )
    pl.semaphore_wait(barrier, 4)

    weight_copies = [
        remote(mine, theirs, twin_send.at[k], twin_recv.at[k], twin)
        for k, (mine, theirs) in enumerate(
            ((w_key, twin_key), (value_weight, twin_value), (w_query, twin_query))
        )
    ]
    for copy in weight_copies:
        copy.start()

    @pl.loop(0, context.shape[0] // 16)
    def _(index):
        first = pl.multiple_of(index * 16, 16)
        rows = normalize_rows(context, gain, first, 16)
        for k in range(4):
            sliced[k, pl.ds(first, 16), :] = rows[:, k * 1024 : (k + 1) * 1024]

    row_copies = [
        remote(
            sliced.at[peer(step)], gathered.at[step, pl.ds(0, 128)], row_send.at[step],
            row_recv.at[step], peer(step) * 2 + core,
        )
        for step in range(3)
    ]
    for step in (2, 0, 1):
        row_copies[step].start()

    @pl.loop(0, query_acts.shape[0] // 16)
    def _(index):
        first = pl.multiple_of(index * 16, 16)
        rows = normalize_rows(query_acts, gain, first, 16)
        for k in range(4):
            query_sliced[k, pl.ds(first, 16), :] = rows[:, k * 1024 : (k + 1) * 1024]

    gathered[3, 0:128] = sliced[chip]
    for step in range(4):
        first = pl.multiple_of(peer(step) * 16, 16)
        gathered[step, 128:144] = query_sliced[chip, pl.ds(first, 16), :]

    for copy in weight_copies:
        copy.wait()

    def sum_copy(step, k):
        return remote(
            partial.at[step, k], arrived.at[step, k], sum_send.at[step, k], sum_recv.at[step, k],
            peer(step) * 2 + core,
        )

    def multiply(step):
        own_rows = gathered[step, :, pl.ds(pl.multiple_of(core * 512, 512), 512)]
        twin_rows = gathered[step, :, pl.ds(pl.multiple_of((1 - core) * 512, 512), 512)]
        for k in range(6):
            if k < 2:
                own_tile = (w_key, value_weight)[k][...]
                twin_tile = (twin_key, twin_value)[k][...]
            else:
                own_tile = w_query[:, (k - 2) * 512 : (k - 1) * 512]
                twin_tile = twin_query[:, (k - 2) * 512 : (k - 1) * 512]
            partial[step, k] = jnp.dot(
                own_rows, own_tile, preferred_element_type=jnp.float32
            ) + jnp.dot(twin_rows, twin_tile, preferred_element_type=jnp.float32)

            @pl.when(step < 3)
            def _():
                sum_copy(step, k).start()

    for step in range(3):
        row_copies[step].wait()
    lax.fori_loop(0, 4, lambda step, carry: (multiply(step), carry)[1], 0)

    for k in range(6):
        for step in range(3):
            sum_copy(step, k).wait()
        total = partial[3, k] + arrived[0, k] + arrived[1, k] + arrived[2, k]
        rounded = total.astype(jnp.bfloat16)
        context_out[:, k * 512 : (k + 1) * 512] = rounded[0:128]
        own_query[:, k * 512 : (k + 1) * 512] = rounded[128:144]

    query_copies = [
        remote(
            own_query, peer_query.at[step], query_send.at[step], query_recv.at[step],
            peer(step) * 2 + core,
        )
        for step in range(3)
    ]
    for copy in query_copies:
        copy.start()
    query_out[pl.ds(pl.multiple_of(chip * 16, 16), 16), :] = own_query[...]
    for step in range(3):
        query_copies[step].wait()
        query_out[pl.ds(pl.multiple_of(peer(step) * 16, 16), 16), :] = peer_query[step]


def project(context, query_acts, norm_gain, w_query, w_key, value_weight):
    vmem = pl.BlockSpec(memory_space=pltpu.VMEM)
    bf16, f32, dma = jnp.bfloat16, jnp.float32, pltpu.SemaphoreType.DMA
    return pl.pallas_call(
        projection_kernel,
        out_shape=[
            jax.ShapeDtypeStruct((128, 3072), bf16),
            jax.ShapeDtypeStruct((64, 3072), bf16),
        ],
        in_specs=[vmem] * 6,
        out_specs=[vmem] * 2,
        scratch_shapes=[
            pltpu.VMEM((512, 2048), bf16),
            pltpu.VMEM((512, 512), bf16),
            pltpu.VMEM((512, 512), bf16),
            pltpu.VMEM((4, 128, 1024), bf16),
            pltpu.VMEM((4, 64, 1024), bf16),
            pltpu.VMEM((4, 144, 1024), bf16),
            pltpu.VMEM((4, 6, 144, 512), f32),
            pltpu.VMEM((3, 6, 144, 512), f32),
            pltpu.VMEM((16, 3072), bf16),
            pltpu.VMEM((3, 16, 3072), bf16),
            dma((3,)), dma((3,)), dma((3,)), dma((3,)), dma((3, 6)), dma((3, 6)), dma((3,)), dma((3,)),
        ],
        compiler_params=pltpu.CompilerParams(
            collective_id=0, has_side_effects=True, vmem_limit_bytes=56 * 2**20
        ),
        cost_estimate=pl.CostEstimate(flops=4 * 144 * 1024 * 3072 * 2, bytes_accessed=8 * 2**20, transcendentals=0),
    )(context, query_acts, norm_gain.reshape(1, -1), w_query, w_key, value_weight)


def attend_part(query_rows, key_row_block, value_matrix, allowed):
    count_of_rows = query_rows.shape[0]
    head_groups = query_rows.reshape(
        count_of_rows, KEY_VALUE_HEADS, QUERY_HEADS // KEY_VALUE_HEADS, HEAD_SIZE
    )
    per_head_keys = key_row_block.reshape(key_row_block.shape[0], KEY_VALUE_HEADS, HEAD_SIZE)
    per_head_values = value_matrix.reshape(value_matrix.shape[0], KEY_VALUE_HEADS, HEAD_SIZE)
    scores = jnp.einsum(
        "rhgd,khd->hgrk", head_groups, per_head_keys, preferred_element_type=jnp.float32
    ) * HEAD_SIZE ** (-0.5)
    scores = jnp.where(allowed, scores, -jnp.inf)
    maxima = jnp.max(scores, axis=-1)
    weights = jnp.exp(scores - maxima[..., None])
    sum_exp = jnp.sum(weights, axis=-1)
    numerator = jnp.einsum(
        "hgrk,khd->rhgd",
        weights.astype(jnp.bfloat16),
        per_head_values,
        preferred_element_type=jnp.float32,
    )
    return (
        maxima.reshape(QUERY_HEADS, count_of_rows),
        sum_exp.reshape(QUERY_HEADS, count_of_rows),
        numerator.reshape(count_of_rows, QUERY_HEADS * HEAD_SIZE),
    )


def spread(factor):
    return jnp.repeat(factor.T, HEAD_SIZE, axis=1)


def combine(former, latter):
    maxima = jnp.maximum(former[0], latter[0])
    scale_one = jnp.exp(former[0] - maxima)
    scale_two = jnp.exp(latter[0] - maxima)
    return (
        maxima,
        former[1] * scale_one + latter[1] * scale_two,
        former[2] * spread(scale_one) + latter[2] * spread(scale_two),
    )


def finish(pieces):
    return (pieces[2] / spread(pieces[1])).astype(jnp.bfloat16)


def share_anchor(stacked):
    return broadcast(stacked, ("outer", "inner"), 0)


def project_all(context, query_acts, norm_gain, w_query, w_key, value_weight):
    if lax.axis_size("inner") == 8:
        rows, queries = project(context, query_acts, norm_gain, w_query, w_key, value_weight)
        both = jnp.concatenate([rows, queries], axis=0)
        return both[:, 1024:], both[:, :512], both[:, 512:1024]
    normed = jnp.concatenate(
        [normalize(context, norm_gain), normalize(query_acts, norm_gain)], axis=0
    )
    return tuple(
        jnp.dot(
            normed,
            lax.all_gather(weight, "inner", axis=0, tiled=True),
            preferred_element_type=jnp.float32,
        ).astype(jnp.bfloat16)
        for weight in (w_query, w_key, value_weight)
    )


def per_device(context, query_acts, norm_gain, w_query, w_key, value_weight, lengths):
    block_rows = context.shape[0]
    projected_q, projected_k, projected_v = project_all(
        context, query_acts, norm_gain, w_query, w_key, value_weight
    )
    anchor = share_anchor(jnp.stack([projected_k[:block_rows], projected_v[:block_rows]]))
    position = lax.axis_index(("outer", "inner"))
    own_length = lengths[position]
    anchor_length = lengths[0]
    places = jnp.arange(block_rows, dtype=jnp.int32)
    causal = places[:, None] >= places[None, :]
    block_q = projected_q[:block_rows]
    block_k = projected_k[:block_rows]
    block_v = projected_v[:block_rows]
    query_q = projected_q[block_rows:]
    query_k = projected_k[block_rows:]
    query_v = projected_v[block_rows:]
    query_count = query_q.shape[0]
    own_allowed = causal & (places[None, :] < own_length)
    anchor_allowed = jnp.broadcast_to(
        (places[None, :] < anchor_length) & (position > 0), (block_rows, block_rows)
    )
    allowed = jnp.concatenate([anchor_allowed, own_allowed], axis=1)
    key_row_block = jnp.concatenate([anchor[0], block_k], axis=0)
    value_rows = jnp.concatenate([anchor[1], block_v], axis=0)
    block_out = finish(attend_part(block_q, key_row_block, value_rows, allowed))
    reached = jnp.broadcast_to(places[None, :] < own_length, (query_count, block_rows))
    block_part = attend_part(query_q, block_k, block_v, reached)
    highest = lax.pmax(block_part[0], ("outer", "inner"))
    rescale = jnp.exp(block_part[0] - highest)
    summed_parts = lax.psum(
        (block_part[1] * rescale, block_part[2] * spread(rescale)), ("outer", "inner")
    )
    merged = (highest, summed_parts[0], summed_parts[1])
    query_places = jnp.arange(query_count, dtype=jnp.int32)
    self_part = attend_part(
        query_q, query_k, query_v, query_places[:, None] >= query_places[None, :]
    )
    return (block_out, finish(combine(merged, self_part)))


def solution(mesh):
    in_specs = (
        P(("outer", "inner"), None),
        P(),
        P(),
        P("inner", None),
        P("inner", None),
        P("inner", None),
        P(),
    )
    out_specs = (P(("outer", "inner"), None), P())
    return jax.shard_map(
        per_device, mesh=mesh, in_specs=in_specs, out_specs=out_specs, check_vma=False
    )
```

```python
import jax
import jax.numpy as jnp
from jax import lax
from jax.experimental import pallas as pl
from jax.experimental.pallas import tpu as pltpu
from jax.sharding import PartitionSpec as P

QUERY_HEADS = 16
KEY_VALUE_HEADS = 4
HEAD_SIZE = 128


epsilon = 1e-05


def broadcast(block, axis, owner):
    block = jnp.where(lax.axis_index(axis) == owner, block, jnp.zeros_like(block))
    return lax.psum(block, axis)


def normalize(matrix, norm_gain):
    widened = matrix.astype(jnp.float32)
    factor = lax.rsqrt(jnp.mean(widened * widened, axis=-1, keepdims=True) + epsilon)
    return (widened * factor * norm_gain).astype(jnp.bfloat16)


def chip_peer(chip, step):
    offset = (step + 1) % 4
    return (chip // 2 + offset // 2) % 2 * 2 + (chip + offset) % 2


def normalize_rows(source, gain, first, count):
    widened = source[pl.ds(first, count), :].astype(jnp.float32)
    factor = lax.rsqrt(jnp.mean(widened * widened, axis=-1, keepdims=True) + epsilon)
    return (widened * factor * gain[...]).astype(jnp.bfloat16)


def projection_kernel(
    context, query_acts, gain, w_query, w_key, value_weight, context_out, query_out,
    twin_query, twin_key, twin_value, sliced, query_sliced, gathered, partial, arrived,
    own_query, peer_query, twin_send, twin_recv, row_send, row_recv, sum_send, sum_recv,
    query_send, query_recv,
):
    inner = lax.axis_index("inner")
    chip, core = inner // 2, inner % 2
    twin = chip * 2 + 1 - core

    def peer(step):
        return chip_peer(chip, step)

    def remote(source, target, send, recv, device):
        return pltpu.make_async_remote_copy(
            src_ref=source, dst_ref=target, send_sem=send, recv_sem=recv,
            device_id={"inner": device}, device_id_type=pl.DeviceIdType.MESH,
        )

    barrier = pltpu.get_barrier_semaphore()
    pl.semaphore_signal(barrier, inc=1, device_id={"inner": twin}, device_id_type=pl.DeviceIdType.MESH)
    for step in range(3):
        pl.semaphore_signal(
            barrier, inc=1, device_id={"inner": peer(step) * 2 + core},
            device_id_type=pl.DeviceIdType.MESH,
        )
    pl.semaphore_wait(barrier, 4)

    weight_copies = [
        remote(mine, theirs, twin_send.at[k], twin_recv.at[k], twin)
        for k, (mine, theirs) in enumerate(
            ((w_key, twin_key), (value_weight, twin_value), (w_query, twin_query))
        )
    ]
    for copy in weight_copies:
        copy.start()

    @pl.loop(0, context.shape[0] // 16)
    def _(index):
        first = pl.multiple_of(index * 16, 16)
        rows = normalize_rows(context, gain, first, 16)
        for k in range(4):
            sliced[k, pl.ds(first, 16), :] = rows[:, k * 1024 : (k + 1) * 1024]

    row_copies = [
        remote(
            sliced.at[peer(step)], gathered.at[step, pl.ds(0, 128)], row_send.at[step],
            row_recv.at[step], peer(step) * 2 + core,
        )
        for step in range(3)
    ]
    for step in (2, 0, 1):
        row_copies[step].start()

    @pl.loop(0, query_acts.shape[0] // 16)
    def _(index):
        first = pl.multiple_of(index * 16, 16)
        rows = normalize_rows(query_acts, gain, first, 16)
        for k in range(4):
            query_sliced[k, pl.ds(first, 16), :] = rows[:, k * 1024 : (k + 1) * 1024]

    gathered[3, 0:128] = sliced[chip]
    for step in range(4):
        first = pl.multiple_of(peer(step) * 16, 16)
        gathered[step, 128:144] = query_sliced[chip, pl.ds(first, 16), :]

    for copy in weight_copies:
        copy.wait()

    def sum_copy(step, k):
        return remote(
            partial.at[step, k], arrived.at[step, k], sum_send.at[step, k], sum_recv.at[step, k],
            peer(step) * 2 + core,
        )

    def multiply(step):
        own_rows = gathered[step, :, pl.ds(pl.multiple_of(core * 512, 512), 512)]
        twin_rows = gathered[step, :, pl.ds(pl.multiple_of((1 - core) * 512, 512), 512)]
        for k in range(6):
            if k < 2:
                own_tile = (w_key, value_weight)[k][...]
                twin_tile = (twin_key, twin_value)[k][...]
            else:
                own_tile = w_query[:, (k - 2) * 512 : (k - 1) * 512]
                twin_tile = twin_query[:, (k - 2) * 512 : (k - 1) * 512]
            partial[step, k] = jnp.dot(
                own_rows, own_tile, preferred_element_type=jnp.float32
            ) + jnp.dot(twin_rows, twin_tile, preferred_element_type=jnp.float32)

            @pl.when(step < 3)
            def _():
                sum_copy(step, k).start()

    for step in range(3):
        row_copies[step].wait()
    lax.fori_loop(0, 4, lambda step, carry: (multiply(step), carry)[1], 0)

    for k in range(6):
        for step in range(3):
            sum_copy(step, k).wait()
        total = partial[3, k] + arrived[0, k] + arrived[1, k] + arrived[2, k]
        rounded = total.astype(jnp.bfloat16)
        context_out[:, k * 512 : (k + 1) * 512] = rounded[0:128]
        own_query[:, k * 512 : (k + 1) * 512] = rounded[128:144]

    query_copies = [
        remote(
            own_query, peer_query.at[step], query_send.at[step], query_recv.at[step],
            peer(step) * 2 + core,
        )
        for step in range(3)
    ]
    for copy in query_copies:
        copy.start()
    query_out[pl.ds(pl.multiple_of(chip * 16, 16), 16), :] = own_query[...]
    for step in range(3):
        query_copies[step].wait()
        query_out[pl.ds(pl.multiple_of(peer(step) * 16, 16), 16), :] = peer_query[step]


def project(context, query_acts, norm_gain, w_query, w_key, value_weight):
    vmem = pl.BlockSpec(memory_space=pltpu.VMEM)
    bf16, f32, dma = jnp.bfloat16, jnp.float32, pltpu.SemaphoreType.DMA
    return pl.pallas_call(
        projection_kernel,
        out_shape=[
            jax.ShapeDtypeStruct((128, 3072), bf16),
            jax.ShapeDtypeStruct((64, 3072), bf16),
        ],
        in_specs=[vmem] * 6,
        out_specs=[vmem] * 2,
        scratch_shapes=[
            pltpu.VMEM((512, 2048), bf16),
            pltpu.VMEM((512, 512), bf16),
            pltpu.VMEM((512, 512), bf16),
            pltpu.VMEM((4, 128, 1024), bf16),
            pltpu.VMEM((4, 64, 1024), bf16),
            pltpu.VMEM((4, 144, 1024), bf16),
            pltpu.VMEM((4, 6, 144, 512), f32),
            pltpu.VMEM((3, 6, 144, 512), f32),
            pltpu.VMEM((16, 3072), bf16),
            pltpu.VMEM((3, 16, 3072), bf16),
            dma((3,)), dma((3,)), dma((3,)), dma((3,)), dma((3, 6)), dma((3, 6)), dma((3,)), dma((3,)),
        ],
        compiler_params=pltpu.CompilerParams(
            collective_id=0, has_side_effects=True, vmem_limit_bytes=56 * 2**20
        ),
        cost_estimate=pl.CostEstimate(flops=4 * 144 * 1024 * 3072 * 2, bytes_accessed=8 * 2**20, transcendentals=0),
    )(context, query_acts, norm_gain.reshape(1, -1), w_query, w_key, value_weight)


def masked_softmax(rows, keys, values, allowed):
    scores = lax.dot_general(
        rows, keys, (((1,), (1,)), ((), ())), preferred_element_type=jnp.float32
    ) * HEAD_SIZE ** (-0.5)
    scores = jnp.where(allowed, scores, -jnp.inf)
    peak = jnp.max(scores, axis=-1, keepdims=True)
    weights = jnp.exp(scores - peak)
    sum_exp = jnp.sum(weights, axis=-1, keepdims=True)
    numerator = jnp.dot(
        weights.astype(jnp.bfloat16), values, preferred_element_type=jnp.float32
    )
    return peak, sum_exp, numerator


def iota(shape, dim):
    return lax.broadcasted_iota(jnp.int32, shape, dim)


def head_rows(source, head_group):
    first = 1024 + head_group * 512
    return jnp.concatenate(
        [source[:, first + g * 128 : first + (g + 1) * 128] for g in range(4)], axis=0
    )


def store_partials(target, head_group, partials):
    peak, sum_exp, numerator = partials
    row, lane = iota((32, 128), 0), iota((32, 128), 1)
    for b in range(8):
        part = slice(b * 32, (b + 1) * 32)
        target[head_group * 8 + b, 0:32] = numerator[part]
        stats = jnp.where(lane == row, peak[part], 0.0) + jnp.where(
            lane == row + 32, sum_exp[part], 0.0
        )
        target[head_group * 8 + b, 32:40] = jnp.broadcast_to(
            jnp.sum(stats, axis=0, keepdims=True), (8, 128)
        )


def stat_column(stats, shift):
    row, lane = iota((32, 128), 0), iota((32, 128), 1)
    spread_stats = jnp.broadcast_to(stats, (32, 128))
    return jnp.sum(
        jnp.where(lane == row + shift, spread_stats, 0.0), axis=1, keepdims=True
    )


def attention_kernel(
    context, query, lengths, block_out, query_out,
    anchor, partials, own_partials, received, merged, merged_all,
    scatter_send, column_send, plane_send, anchor_recv,
    partial_send, partial_recv, merged_send, merged_recv,
):
    outer, inner = lax.axis_index("outer"), lax.axis_index("inner")
    outers, inners = lax.axis_size("outer"), lax.axis_size("inner")
    devices = outers * inners
    me = outer * inners + inner

    def remote(source, target, send, recv, to_outer, to_inner):
        return pltpu.make_async_remote_copy(
            src_ref=source, dst_ref=target, send_sem=send, recv_sem=recv,
            device_id={"outer": to_outer, "inner": to_inner},
            device_id_type=pl.DeviceIdType.MESH,
        )

    barrier = pltpu.get_barrier_semaphore()

    def greet(t, carry):
        other = (me + t) % devices
        pl.semaphore_signal(
            barrier, inc=1, device_id={"outer": other // inners, "inner": other % inners},
            device_id_type=pl.DeviceIdType.MESH,
        )
        return carry

    lax.fori_loop(1, devices, greet, 0)
    pl.semaphore_wait(barrier, devices - 1)

    def scatter_copy(j):
        return remote(
            context.at[:, pl.ds(j * 128, 128)], anchor.at[j], scatter_send.at[j],
            anchor_recv.at[j], 0, j,
        )

    @pl.when(me == 0)
    def _():
        for j in range(1, 8):
            scatter_copy(j).start()
        anchor[0] = context[:, 0:128]

    own_length, anchor_length = lengths[me], lengths[0]

    for h in range(4):
        keys = context[:, h * 128 : (h + 1) * 128]
        values = context[:, 512 + h * 128 : 512 + (h + 1) * 128]
        reached = iota((256, 128), 1) < own_length
        store_partials(partials, h, masked_softmax(head_rows(query, h), keys, values, reached))

    def partial_copy(other):
        return lambda slot: remote(
            partials.at[other], received.at[slot], partial_send.at[other], partial_recv.at[slot],
            other // inners, other % inners,
        )

    def send_partial(t, carry):
        partial_copy((me + t) % devices)(me).start()
        return carry

    lax.fori_loop(1, devices, send_partial, 0)

    def column_copy(o):
        return remote(
            anchor.at[inner], anchor.at[inner], column_send.at[o], anchor_recv.at[inner], o, inner
        )

    def plane_copy(j, slot):
        return remote(
            anchor.at[slot], anchor.at[slot], plane_send.at[j], anchor_recv.at[slot], outer, j
        )

    @pl.when(me != 0)
    def _():
        plane_copy(inner, inner).wait_recv()

    @pl.when(outer == 0)
    def _():
        for o in range(1, 4):
            column_copy(o).start()

    def send_plane(t, carry):
        plane_copy((inner + t) % inners, inner).start()
        return carry

    lax.fori_loop(1, inners, send_plane, 0)

    for h in range(4):
        keys = query[:, h * 128 : (h + 1) * 128]
        values = query[:, 512 + h * 128 : 512 + (h + 1) * 128]
        causal = iota((256, 64), 0) % 64 >= iota((256, 64), 1)
        store_partials(own_partials, h, masked_softmax(head_rows(query, h), keys, values, causal))
    received[me] = partials[me]
    received[devices] = own_partials[me]

    def wait_plane(t, carry):
        other = (inner + t) % inners
        plane_copy(other, inner).wait_send()
        plane_copy(other, other).wait_recv()
        return carry

    lax.fori_loop(1, inners, wait_plane, 0)

    row, column = iota((512, 256), 0) % 128, iota((512, 256), 1)
    place = column % 128
    limit = jnp.where(column < 128, jnp.where(me > 0, anchor_length, 0), own_length)
    allowed = (place < limit) & ((column < 128) | (row >= place))
    for h in range(4):
        keys = jnp.concatenate([anchor[h], context[:, h * 128 : (h + 1) * 128]], axis=0)
        values = jnp.concatenate(
            [anchor[4 + h], context[:, 512 + h * 128 : 512 + (h + 1) * 128]], axis=0
        )
        _, sum_exp, numerator = masked_softmax(head_rows(context, h), keys, values, allowed)
        result = (numerator / sum_exp).astype(jnp.bfloat16)
        for g in range(4):
            block_out[:, (h * 4 + g) * 128 : (h * 4 + g + 1) * 128] = result[
                g * 128 : (g + 1) * 128
            ]

    def wait_partial(t, carry):
        other = (me + t) % devices
        partial_copy(other)(other).wait()
        return carry

    lax.fori_loop(1, devices, wait_partial, 0)

    def highest(s, peak):
        return jnp.maximum(peak, stat_column(received[s, 32:33], 0))

    top = lax.fori_loop(
        0, devices + 1, highest, jnp.full((32, 1), -jnp.inf, jnp.float32)
    )

    def add_up(s, carry):
        total, numerator = carry
        factor = jnp.exp(stat_column(received[s, 32:33], 0) - top)
        return (
            total + stat_column(received[s, 32:33], 32) * factor,
            numerator + received[s, 0:32] * factor,
        )

    total, numerator = lax.fori_loop(
        0, devices + 1, add_up,
        (jnp.zeros((32, 1), jnp.float32), jnp.zeros((32, 128), jnp.float32)),
    )
    merged[...] = (numerator / total).astype(jnp.bfloat16)

    def merged_copy(other, slot):
        return remote(
            merged, merged_all.at[slot], merged_send.at[other], merged_recv.at[slot],
            other // inners, other % inners,
        )

    def send_merged(t, carry):
        merged_copy((me + t) % devices, me).start()
        return carry

    lax.fori_loop(1, devices, send_merged, 0)
    merged_all[me] = merged[...]

    @pl.when(me == 0)
    def _():
        for j in range(1, 8):
            scatter_copy(j).wait_send()

    @pl.when(outer == 0)
    def _():
        for o in range(1, 4):
            column_copy(o).wait_send()

    def wait_merged(t, carry):
        other = (me + t) % devices
        merged_copy(other, other).wait()
        return carry

    lax.fori_loop(1, devices, wait_merged, 0)
    for d in range(32):
        query_out[d % 2 * 32 : d % 2 * 32 + 32, d // 2 * 128 : d // 2 * 128 + 128] = merged_all[d]


def attend(context, query, lengths):
    vmem = pl.BlockSpec(memory_space=pltpu.VMEM)
    bf16, f32, dma = jnp.bfloat16, jnp.float32, pltpu.SemaphoreType.DMA
    return pl.pallas_call(
        attention_kernel,
        out_shape=[
            jax.ShapeDtypeStruct((128, 2048), bf16),
            jax.ShapeDtypeStruct((64, 2048), bf16),
        ],
        in_specs=[vmem, vmem, pl.BlockSpec(memory_space=pltpu.SMEM)],
        out_specs=[vmem] * 2,
        scratch_shapes=[
            pltpu.VMEM((8, 128, 128), bf16),
            pltpu.VMEM((32, 40, 128), f32),
            pltpu.VMEM((32, 40, 128), f32),
            pltpu.VMEM((33, 40, 128), f32),
            pltpu.VMEM((32, 128), bf16),
            pltpu.VMEM((32, 32, 128), bf16),
            dma((8,)), dma((4,)), dma((8,)), dma((8,)),
            dma((32,)), dma((32,)), dma((32,)), dma((32,)),
        ],
        compiler_params=pltpu.CompilerParams(
            collective_id=1, has_side_effects=True, vmem_limit_bytes=48 * 2**20
        ),
        cost_estimate=pl.CostEstimate(flops=10**9, bytes_accessed=4 * 2**20, transcendentals=10**6),
    )(context, query, lengths)


def attend_part(query_rows, key_row_block, value_matrix, allowed):
    count_of_rows = query_rows.shape[0]
    head_groups = query_rows.reshape(
        count_of_rows, KEY_VALUE_HEADS, QUERY_HEADS // KEY_VALUE_HEADS, HEAD_SIZE
    )
    per_head_keys = key_row_block.reshape(key_row_block.shape[0], KEY_VALUE_HEADS, HEAD_SIZE)
    per_head_values = value_matrix.reshape(value_matrix.shape[0], KEY_VALUE_HEADS, HEAD_SIZE)
    scores = jnp.einsum(
        "rhgd,khd->hgrk", head_groups, per_head_keys, preferred_element_type=jnp.float32
    ) * HEAD_SIZE ** (-0.5)
    scores = jnp.where(allowed, scores, -jnp.inf)
    maxima = jnp.max(scores, axis=-1)
    weights = jnp.exp(scores - maxima[..., None])
    sum_exp = jnp.sum(weights, axis=-1)
    numerator = jnp.einsum(
        "hgrk,khd->rhgd",
        weights.astype(jnp.bfloat16),
        per_head_values,
        preferred_element_type=jnp.float32,
    )
    return (
        maxima.reshape(QUERY_HEADS, count_of_rows),
        sum_exp.reshape(QUERY_HEADS, count_of_rows),
        numerator.reshape(count_of_rows, QUERY_HEADS * HEAD_SIZE),
    )


def spread(factor):
    return jnp.repeat(factor.T, HEAD_SIZE, axis=1)


def combine(former, latter):
    maxima = jnp.maximum(former[0], latter[0])
    scale_one = jnp.exp(former[0] - maxima)
    scale_two = jnp.exp(latter[0] - maxima)
    return (
        maxima,
        former[1] * scale_one + latter[1] * scale_two,
        former[2] * spread(scale_one) + latter[2] * spread(scale_two),
    )


def finish(pieces):
    return (pieces[2] / spread(pieces[1])).astype(jnp.bfloat16)


def share_anchor(stacked):
    return broadcast(stacked, ("outer", "inner"), 0)


def project_all(context, query_acts, norm_gain, w_query, w_key, value_weight):
    normed = jnp.concatenate(
        [normalize(context, norm_gain), normalize(query_acts, norm_gain)], axis=0
    )
    return tuple(
        jnp.dot(
            normed,
            lax.all_gather(weight, "inner", axis=0, tiled=True),
            preferred_element_type=jnp.float32,
        ).astype(jnp.bfloat16)
        for weight in (w_query, w_key, value_weight)
    )


def per_device(context, query_acts, norm_gain, w_query, w_key, value_weight, lengths):
    if (lax.axis_size("outer"), lax.axis_size("inner")) == (4, 8):
        rows, queries = project(context, query_acts, norm_gain, w_query, w_key, value_weight)
        return tuple(attend(rows, queries, lengths))
    block_rows = context.shape[0]
    projected_q, projected_k, projected_v = project_all(
        context, query_acts, norm_gain, w_query, w_key, value_weight
    )
    anchor = share_anchor(jnp.stack([projected_k[:block_rows], projected_v[:block_rows]]))
    position = lax.axis_index(("outer", "inner"))
    own_length = lengths[position]
    anchor_length = lengths[0]
    places = jnp.arange(block_rows, dtype=jnp.int32)
    causal = places[:, None] >= places[None, :]
    block_q = projected_q[:block_rows]
    block_k = projected_k[:block_rows]
    block_v = projected_v[:block_rows]
    query_q = projected_q[block_rows:]
    query_k = projected_k[block_rows:]
    query_v = projected_v[block_rows:]
    query_count = query_q.shape[0]
    own_allowed = causal & (places[None, :] < own_length)
    anchor_allowed = jnp.broadcast_to(
        (places[None, :] < anchor_length) & (position > 0), (block_rows, block_rows)
    )
    allowed = jnp.concatenate([anchor_allowed, own_allowed], axis=1)
    key_row_block = jnp.concatenate([anchor[0], block_k], axis=0)
    value_rows = jnp.concatenate([anchor[1], block_v], axis=0)
    block_out = finish(attend_part(block_q, key_row_block, value_rows, allowed))
    reached = jnp.broadcast_to(places[None, :] < own_length, (query_count, block_rows))
    block_part = attend_part(query_q, block_k, block_v, reached)
    highest = lax.pmax(block_part[0], ("outer", "inner"))
    rescale = jnp.exp(block_part[0] - highest)
    summed_parts = lax.psum(
        (block_part[1] * rescale, block_part[2] * spread(rescale)), ("outer", "inner")
    )
    merged = (highest, summed_parts[0], summed_parts[1])
    query_places = jnp.arange(query_count, dtype=jnp.int32)
    self_part = attend_part(
        query_q, query_k, query_v, query_places[:, None] >= query_places[None, :]
    )
    return (block_out, finish(combine(merged, self_part)))


def solution(mesh):
    in_specs = (
        P(("outer", "inner"), None),
        P(),
        P(),
        P("inner", None),
        P("inner", None),
        P("inner", None),
        P(),
    )
    out_specs = (P(("outer", "inner"), None), P())
    return jax.shard_map(
        per_device, mesh=mesh, in_specs=in_specs, out_specs=out_specs, check_vma=False
    )
```

```python
import jax
import jax.numpy as jnp
from jax import lax
from jax.experimental import pallas as pl
from jax.experimental.pallas import tpu as pltpu
from jax.sharding import PartitionSpec as P

QUERY_HEADS = 16
KEY_VALUE_HEADS = 4
HEAD_SIZE = 128


epsilon = 1e-05


def broadcast(block, axis, owner):
    block = jnp.where(lax.axis_index(axis) == owner, block, jnp.zeros_like(block))
    return lax.psum(block, axis)


def normalize(matrix, norm_gain):
    widened = matrix.astype(jnp.float32)
    factor = lax.rsqrt(jnp.mean(widened * widened, axis=-1, keepdims=True) + epsilon)
    return (widened * factor * norm_gain).astype(jnp.bfloat16)


def chip_peer(chip, step):
    offset = (step + 1) % 4
    return (chip // 2 + offset // 2) % 2 * 2 + (chip + offset) % 2


def normalize_rows(source, gain, first, count):
    widened = source[pl.ds(first, count), :].astype(jnp.float32)
    factor = lax.rsqrt(jnp.mean(widened * widened, axis=-1, keepdims=True) + epsilon)
    return (widened * factor * gain[...]).astype(jnp.bfloat16)


def masked_softmax(rows, keys, values, allowed):
    scores = lax.dot_general(
        rows, keys, (((1,), (1,)), ((), ())), preferred_element_type=jnp.float32
    ) * HEAD_SIZE ** (-0.5)
    scores = jnp.where(allowed, scores, -jnp.inf)
    peak = jnp.max(scores, axis=-1, keepdims=True)
    weights = jnp.exp(scores - peak)
    sum_exp = jnp.sum(weights, axis=-1, keepdims=True)
    numerator = jnp.dot(
        weights.astype(jnp.bfloat16), values, preferred_element_type=jnp.float32
    )
    return peak, sum_exp, numerator


def iota(shape, dim):
    return lax.broadcasted_iota(jnp.int32, shape, dim)


def head_rows(source, head_group):
    first = 1024 + head_group * 512
    return jnp.concatenate(
        [source[:, first + g * 128 : first + (g + 1) * 128] for g in range(4)], axis=0
    )


def store_partials(target, head_group, partials):
    peak, sum_exp, numerator = partials
    row, lane = iota((32, 128), 0), iota((32, 128), 1)
    for b in range(8):
        part = slice(b * 32, (b + 1) * 32)
        target[head_group * 8 + b, 0:32] = numerator[part]
        stats = jnp.where(lane == row, peak[part], 0.0) + jnp.where(
            lane == row + 32, sum_exp[part], 0.0
        )
        target[head_group * 8 + b, 32:40] = jnp.broadcast_to(
            jnp.sum(stats, axis=0, keepdims=True), (8, 128)
        )


def stat_column(stats, shift):
    row, lane = iota((32, 128), 0), iota((32, 128), 1)
    spread_stats = jnp.broadcast_to(stats, (32, 128))
    return jnp.sum(
        jnp.where(lane == row + shift, spread_stats, 0.0), axis=1, keepdims=True
    )


def layer_kernel(
    context_rows, query_acts, gain, w_query, w_key, value_weight, lengths, block_out, query_out,
    twin_query, twin_key, twin_value, sliced, query_sliced, gathered, partial, first_sum, passed,
    second_sum, query_sums, query_arrived, query_mine, query_parts, context, query,
    anchor, partials, own_partials, received, merged, merged_all,
    twin_send, twin_recv, row_send, row_recv, first_send, first_recv, passed_send, passed_recv,
    second_send, second_recv, query_send, query_recv, spread_send, spread_recv,
    scatter_send, column_send, plane_send, anchor_recv,
    partial_send, partial_recv, merged_send, merged_recv,
):
    outer, inner = lax.axis_index("outer"), lax.axis_index("inner")
    outers, inners = lax.axis_size("outer"), lax.axis_size("inner")
    devices = outers * inners
    me = outer * inners + inner
    chip, core = inner // 2, inner % 2
    twin = chip * 2 + 1 - core

    def peer(step):
        return chip_peer(chip, step)

    def remote(source, target, send, recv, to_outer, to_inner):
        return pltpu.make_async_remote_copy(
            src_ref=source, dst_ref=target, send_sem=send, recv_sem=recv,
            device_id={"outer": to_outer, "inner": to_inner},
            device_id_type=pl.DeviceIdType.MESH,
        )

    barrier = pltpu.get_barrier_semaphore()

    def greet(t, carry):
        other = (me + t) % devices
        pl.semaphore_signal(
            barrier, inc=1, device_id={"outer": other // inners, "inner": other % inners},
            device_id_type=pl.DeviceIdType.MESH,
        )
        return carry

    lax.fori_loop(1, devices, greet, 0)
    pl.semaphore_wait(barrier, devices - 1)

    weight_copies = [
        remote(mine, theirs, twin_send.at[k], twin_recv.at[k], outer, twin)
        for k, (mine, theirs) in enumerate(
            ((w_key, twin_key), (value_weight, twin_value), (w_query, twin_query))
        )
    ]
    for copy in weight_copies:
        copy.start()

    @pl.loop(0, context_rows.shape[0] // 16)
    def _(index):
        first = pl.multiple_of(index * 16, 16)
        rows = normalize_rows(context_rows, gain, first, 16)
        for k in range(4):
            sliced[k, pl.ds(first, 16), :] = rows[:, k * 1024 : (k + 1) * 1024]

    row_copies = [
        remote(
            sliced.at[peer(step)], gathered.at[step], row_send.at[step], row_recv.at[step],
            outer, peer(step) * 2 + core,
        )
        for step in range(3)
    ]
    for step in (2, 0, 1):
        row_copies[step].start()

    @pl.loop(0, query_acts.shape[0] // 16)
    def _(index):
        first = pl.multiple_of(index * 16, 16)
        rows = normalize_rows(query_acts, gain, first, 16)
        for k in range(4):
            query_sliced[k, pl.ds(first, 16), :] = rows[:, k * 1024 : (k + 1) * 1024]

    gathered[3] = sliced[chip]
    for copy in weight_copies:
        copy.wait()

    def tiles(k):
        if k < 2:
            return (w_key, value_weight)[k][...], (twin_key, twin_value)[k][...]
        columns = slice((k - 2) * 512, (k - 1) * 512)
        return w_query[:, columns], twin_query[:, columns]

    own_columns = pl.ds(pl.multiple_of(core * 512, 512), 512)
    twin_columns = pl.ds(pl.multiple_of((1 - core) * 512, 512), 512)

    def product(source, index, k):
        own_tile, twin_tile = tiles(k)
        return jnp.dot(
            source[index, :, own_columns], own_tile, preferred_element_type=jnp.float32
        ) + jnp.dot(
            source[index, :, twin_columns], twin_tile, preferred_element_type=jnp.float32
        )

    for k in range(6):
        query_sums[:, k * 512 : (k + 1) * 512] = product(query_sliced, chip, k)

    def query_part(other):
        return pl.ds(pl.multiple_of(other * 16 + core * 8, 8), 8)

    query_copies = [
        remote(
            query_sums.at[query_part(peer(step))], query_arrived.at[step], query_send.at[step],
            query_recv.at[step], outer, peer(step) * 2 + core,
        )
        for step in range(3)
    ]
    for copy in query_copies:
        copy.start()

    def first_copy(k):
        return remote(
            partial.at[k % 2, k], first_sum.at[k], first_send.at[k], first_recv.at[k],
            outer, peer(k % 2) * 2 + core,
        )

    def passed_copy(k):
        return remote(
            partial.at[2, k], passed.at[k], passed_send.at[k], passed_recv.at[k],
            outer, peer(k % 2) * 2 + core,
        )

    def second_copy(k):
        return remote(
            partial.at[1 - k % 2, k], second_sum.at[k], second_send.at[k], second_recv.at[k],
            outer, peer(1 - k % 2) * 2 + core,
        )

    def multiply(k):
        def one(step, carry):
            partial[step, k] = product(gathered, step, k)
            return carry

        lax.fori_loop(0, 4, one, 0)
        passed_copy(k).start()
        first_copy(k).start()

    def relay(k):
        passed_copy(k).wait()
        partial[1 - k % 2, k] = partial[1 - k % 2, k] + passed[k]
        second_copy(k).start()

    def settle(k):
        first_copy(k).wait()
        second_copy(k).wait()
        total = partial[3, k] + first_sum[k] + second_sum[k]
        context[:, k * 512 : (k + 1) * 512] = total.astype(jnp.bfloat16)

    for step in range(3):
        row_copies[step].wait()
    for k in range(4):
        multiply(k)

    for copy in query_copies:
        copy.wait()
    query_mine[...] = (
        query_sums[query_part(chip), :] + query_arrived[0] + query_arrived[1] + query_arrived[2]
    ).astype(jnp.bfloat16).astype(jnp.float32)

    def spread_copy(other, slot):
        return remote(
            query_mine, query_parts.at[slot], spread_send.at[other], spread_recv.at[slot],
            outer, other,
        )

    def send_query(t, carry):
        spread_copy((inner + t) % inners, inner).start()
        return carry

    lax.fori_loop(1, inners, send_query, 0)
    query_parts[inner] = query_mine[...]
    relay(0)
    relay(1)
    for k in range(4, 6):
        multiply(k)

    def wait_query(t, carry):
        other = (inner + t) % inners
        spread_copy(other, other).wait()
        return carry

    lax.fori_loop(1, inners, wait_query, 0)
    for pair in range(4):
        query[pair * 16 : (pair + 1) * 16] = jnp.concatenate(
            [query_parts[pair * 2], query_parts[pair * 2 + 1]], axis=0
        ).astype(jnp.bfloat16)
    settle(0)
    settle(1)

    def scatter_copy(j):
        return remote(
            context.at[:, pl.ds(j * 128, 128)], anchor.at[j], scatter_send.at[j],
            anchor_recv.at[j], 0, j,
        )

    @pl.when(me == 0)
    def _():
        for j in range(1, 8):
            scatter_copy(j).start()
        anchor[0] = context[:, 0:128]

    own_length, anchor_length = lengths[me], lengths[0]

    for h in range(4):
        keys = context[:, h * 128 : (h + 1) * 128]
        values = context[:, 512 + h * 128 : 512 + (h + 1) * 128]
        reached = iota((256, 128), 1) < own_length
        store_partials(partials, h, masked_softmax(head_rows(query, h), keys, values, reached))

    def partial_copy(other):
        return lambda slot: remote(
            partials.at[other], received.at[slot], partial_send.at[other], partial_recv.at[slot],
            other // inners, other % inners,
        )

    def send_partial(t, carry):
        partial_copy((me + t) % devices)(me).start()
        return carry

    lax.fori_loop(1, devices, send_partial, 0)

    relay(2)
    relay(3)

    def column_copy(o):
        return remote(
            anchor.at[inner], anchor.at[inner], column_send.at[o], anchor_recv.at[inner], o, inner
        )

    def plane_copy(j, slot):
        return remote(
            anchor.at[slot], anchor.at[slot], plane_send.at[j], anchor_recv.at[slot], outer, j
        )

    @pl.when(me != 0)
    def _():
        plane_copy(inner, inner).wait_recv()

    @pl.when(outer == 0)
    def _():
        for o in range(1, 4):
            column_copy(o).start()

    def send_plane(t, carry):
        plane_copy((inner + t) % inners, inner).start()
        return carry

    lax.fori_loop(1, inners, send_plane, 0)

    for h in range(4):
        keys = query[:, h * 128 : (h + 1) * 128]
        values = query[:, 512 + h * 128 : 512 + (h + 1) * 128]
        causal = iota((256, 64), 0) % 64 >= iota((256, 64), 1)
        store_partials(own_partials, h, masked_softmax(head_rows(query, h), keys, values, causal))
    received[me] = partials[me]
    received[devices] = own_partials[me]

    relay(4)
    relay(5)

    def wait_partial(t, carry):
        other = (me + t) % devices
        partial_copy(other)(other).wait()
        return carry

    lax.fori_loop(1, devices, wait_partial, 0)

    def highest(s, peak):
        return jnp.maximum(peak, stat_column(received[s, 32:33], 0))

    top = lax.fori_loop(
        0, devices + 1, highest, jnp.full((32, 1), -jnp.inf, jnp.float32)
    )

    def add_up(s, carry):
        total, numerator = carry
        factor = jnp.exp(stat_column(received[s, 32:33], 0) - top)
        return (
            total + stat_column(received[s, 32:33], 32) * factor,
            numerator + received[s, 0:32] * factor,
        )

    total, numerator = lax.fori_loop(
        0, devices + 1, add_up,
        (jnp.zeros((32, 1), jnp.float32), jnp.zeros((32, 128), jnp.float32)),
    )
    merged[...] = (numerator / total).astype(jnp.bfloat16)

    def merged_copy(other, slot):
        return remote(
            merged, merged_all.at[slot], merged_send.at[other], merged_recv.at[slot],
            other // inners, other % inners,
        )

    def send_merged(t, carry):
        merged_copy((me + t) % devices, me).start()
        return carry

    lax.fori_loop(1, devices, send_merged, 0)
    merged_all[me] = merged[...]

    for k in range(2, 6):
        settle(k)

    def wait_plane(t, carry):
        other = (inner + t) % inners
        plane_copy(other, inner).wait_send()
        plane_copy(other, other).wait_recv()
        return carry

    lax.fori_loop(1, inners, wait_plane, 0)

    row, column = iota((512, 256), 0) % 128, iota((512, 256), 1)
    place = column % 128
    limit = jnp.where(column < 128, jnp.where(me > 0, anchor_length, 0), own_length)
    allowed = (place < limit) & ((column < 128) | (row >= place))
    for h in range(4):
        keys = jnp.concatenate([anchor[h], context[:, h * 128 : (h + 1) * 128]], axis=0)
        values = jnp.concatenate(
            [anchor[4 + h], context[:, 512 + h * 128 : 512 + (h + 1) * 128]], axis=0
        )
        _, sum_exp, numerator = masked_softmax(head_rows(context, h), keys, values, allowed)
        result = (numerator / sum_exp).astype(jnp.bfloat16)
        for g in range(4):
            block_out[:, (h * 4 + g) * 128 : (h * 4 + g + 1) * 128] = result[
                g * 128 : (g + 1) * 128
            ]

    @pl.when(me == 0)
    def _():
        for j in range(1, 8):
            scatter_copy(j).wait_send()

    @pl.when(outer == 0)
    def _():
        for o in range(1, 4):
            column_copy(o).wait_send()

    def wait_merged(t, carry):
        other = (me + t) % devices
        merged_copy(other, other).wait()
        return carry

    lax.fori_loop(1, devices, wait_merged, 0)
    for d in range(32):
        query_out[d % 2 * 32 : d % 2 * 32 + 32, d // 2 * 128 : d // 2 * 128 + 128] = merged_all[d]


def layer(context, query_acts, norm_gain, w_query, w_key, value_weight, lengths):
    vmem = pl.BlockSpec(memory_space=pltpu.VMEM)
    bf16, f32, dma = jnp.bfloat16, jnp.float32, pltpu.SemaphoreType.DMA
    buffers = [
        ((512, 2048), bf16), ((512, 512), bf16), ((512, 512), bf16),
        ((4, 128, 1024), bf16), ((4, 64, 1024), bf16), ((4, 128, 1024), bf16),
        ((4, 6, 128, 512), f32), ((6, 128, 512), f32), ((6, 128, 512), f32),
        ((6, 128, 512), f32), ((64, 3072), f32), ((3, 8, 3072), f32), ((8, 3072), f32),
        ((8, 8, 3072), f32), ((128, 3072), bf16), ((64, 3072), bf16),
        ((8, 128, 128), bf16), ((32, 40, 128), f32), ((32, 40, 128), f32),
        ((33, 40, 128), f32), ((32, 128), bf16), ((32, 32, 128), bf16),
    ]
    counts = [3, 3, 3, 3, 6, 6, 6, 6, 6, 6, 3, 3, 8, 8, 8, 4, 8, 8, 32, 32, 32, 32]
    return pl.pallas_call(
        layer_kernel,
        out_shape=[
            jax.ShapeDtypeStruct((128, 2048), bf16),
            jax.ShapeDtypeStruct((64, 2048), bf16),
        ],
        in_specs=[vmem] * 6 + [pl.BlockSpec(memory_space=pltpu.SMEM)],
        out_specs=[vmem] * 2,
        scratch_shapes=[pltpu.VMEM(shape, kind) for shape, kind in buffers]
        + [dma((count,)) for count in counts],
        compiler_params=pltpu.CompilerParams(
            collective_id=0, has_side_effects=True, vmem_limit_bytes=56 * 2**20
        ),
        cost_estimate=pl.CostEstimate(
            flops=5 * 10**9, bytes_accessed=8 * 2**20, transcendentals=10**6
        ),
    )(context, query_acts, norm_gain.reshape(1, -1), w_query, w_key, value_weight, lengths)


def attend_part(query_rows, key_row_block, value_matrix, allowed):
    count_of_rows = query_rows.shape[0]
    head_groups = query_rows.reshape(
        count_of_rows, KEY_VALUE_HEADS, QUERY_HEADS // KEY_VALUE_HEADS, HEAD_SIZE
    )
    per_head_keys = key_row_block.reshape(key_row_block.shape[0], KEY_VALUE_HEADS, HEAD_SIZE)
    per_head_values = value_matrix.reshape(value_matrix.shape[0], KEY_VALUE_HEADS, HEAD_SIZE)
    scores = jnp.einsum(
        "rhgd,khd->hgrk", head_groups, per_head_keys, preferred_element_type=jnp.float32
    ) * HEAD_SIZE ** (-0.5)
    scores = jnp.where(allowed, scores, -jnp.inf)
    maxima = jnp.max(scores, axis=-1)
    weights = jnp.exp(scores - maxima[..., None])
    sum_exp = jnp.sum(weights, axis=-1)
    numerator = jnp.einsum(
        "hgrk,khd->rhgd",
        weights.astype(jnp.bfloat16),
        per_head_values,
        preferred_element_type=jnp.float32,
    )
    return (
        maxima.reshape(QUERY_HEADS, count_of_rows),
        sum_exp.reshape(QUERY_HEADS, count_of_rows),
        numerator.reshape(count_of_rows, QUERY_HEADS * HEAD_SIZE),
    )


def spread(factor):
    return jnp.repeat(factor.T, HEAD_SIZE, axis=1)


def combine(former, latter):
    maxima = jnp.maximum(former[0], latter[0])
    scale_one = jnp.exp(former[0] - maxima)
    scale_two = jnp.exp(latter[0] - maxima)
    return (
        maxima,
        former[1] * scale_one + latter[1] * scale_two,
        former[2] * spread(scale_one) + latter[2] * spread(scale_two),
    )


def finish(pieces):
    return (pieces[2] / spread(pieces[1])).astype(jnp.bfloat16)


def share_anchor(stacked):
    return broadcast(stacked, ("outer", "inner"), 0)


def project_all(context, query_acts, norm_gain, w_query, w_key, value_weight):
    normed = jnp.concatenate(
        [normalize(context, norm_gain), normalize(query_acts, norm_gain)], axis=0
    )
    return tuple(
        jnp.dot(
            normed,
            lax.all_gather(weight, "inner", axis=0, tiled=True),
            preferred_element_type=jnp.float32,
        ).astype(jnp.bfloat16)
        for weight in (w_query, w_key, value_weight)
    )


def per_device(context, query_acts, norm_gain, w_query, w_key, value_weight, lengths):
    if (lax.axis_size("outer"), lax.axis_size("inner")) == (4, 8):
        return tuple(
            layer(context, query_acts, norm_gain, w_query, w_key, value_weight, lengths)
        )
    block_rows = context.shape[0]
    projected_q, projected_k, projected_v = project_all(
        context, query_acts, norm_gain, w_query, w_key, value_weight
    )
    anchor = share_anchor(jnp.stack([projected_k[:block_rows], projected_v[:block_rows]]))
    position = lax.axis_index(("outer", "inner"))
    own_length = lengths[position]
    anchor_length = lengths[0]
    places = jnp.arange(block_rows, dtype=jnp.int32)
    causal = places[:, None] >= places[None, :]
    block_q = projected_q[:block_rows]
    block_k = projected_k[:block_rows]
    block_v = projected_v[:block_rows]
    query_q = projected_q[block_rows:]
    query_k = projected_k[block_rows:]
    query_v = projected_v[block_rows:]
    query_count = query_q.shape[0]
    own_allowed = causal & (places[None, :] < own_length)
    anchor_allowed = jnp.broadcast_to(
        (places[None, :] < anchor_length) & (position > 0), (block_rows, block_rows)
    )
    allowed = jnp.concatenate([anchor_allowed, own_allowed], axis=1)
    key_row_block = jnp.concatenate([anchor[0], block_k], axis=0)
    value_rows = jnp.concatenate([anchor[1], block_v], axis=0)
    block_out = finish(attend_part(block_q, key_row_block, value_rows, allowed))
    reached = jnp.broadcast_to(places[None, :] < own_length, (query_count, block_rows))
    block_part = attend_part(query_q, block_k, block_v, reached)
    highest = lax.pmax(block_part[0], ("outer", "inner"))
    rescale = jnp.exp(block_part[0] - highest)
    summed_parts = lax.psum(
        (block_part[1] * rescale, block_part[2] * spread(rescale)), ("outer", "inner")
    )
    merged = (highest, summed_parts[0], summed_parts[1])
    query_places = jnp.arange(query_count, dtype=jnp.int32)
    self_part = attend_part(
        query_q, query_k, query_v, query_places[:, None] >= query_places[None, :]
    )
    return (block_out, finish(combine(merged, self_part)))


def solution(mesh):
    in_specs = (
        P(("outer", "inner"), None),
        P(),
        P(),
        P("inner", None),
        P("inner", None),
        P("inner", None),
        P(),
    )
    out_specs = (P(("outer", "inner"), None), P())
    return jax.shard_map(
        per_device, mesh=mesh, in_specs=in_specs, out_specs=out_specs, check_vma=False
    )
```

```python
import jax
import jax.numpy as jnp
from jax import lax
from jax.experimental import pallas as pl
from jax.experimental.pallas import tpu as pltpu
from jax.sharding import PartitionSpec as P

QUERY_HEADS = 16
KEY_VALUE_HEADS = 4
HEAD_SIZE = 128


epsilon = 1e-05


def broadcast(block, axis, owner):
    block = jnp.where(lax.axis_index(axis) == owner, block, jnp.zeros_like(block))
    return lax.psum(block, axis)


def normalize(matrix, norm_gain):
    widened = matrix.astype(jnp.float32)
    factor = lax.rsqrt(jnp.mean(widened * widened, axis=-1, keepdims=True) + epsilon)
    return (widened * factor * norm_gain).astype(jnp.bfloat16)


def chip_peer(chip, step):
    offset = (step + 1) % 4
    return (chip // 2 + offset // 2) % 2 * 2 + (chip + offset) % 2


def normalize_rows(source, gain, first, count):
    widened = source[pl.ds(first, count), :].astype(jnp.float32)
    factor = lax.rsqrt(jnp.mean(widened * widened, axis=-1, keepdims=True) + epsilon)
    return (widened * factor * gain[...]).astype(jnp.bfloat16)


def masked_softmax(rows, keys, values, allowed):
    scores = lax.dot_general(
        rows, keys, (((1,), (1,)), ((), ())), preferred_element_type=jnp.float32
    ) * HEAD_SIZE ** (-0.5)
    scores = jnp.where(allowed, scores, -jnp.inf)
    peak = jnp.max(scores, axis=-1, keepdims=True)
    weights = jnp.exp(scores - peak)
    sum_exp = jnp.sum(weights, axis=-1, keepdims=True)
    numerator = jnp.dot(
        weights.astype(jnp.bfloat16), values, preferred_element_type=jnp.float32
    )
    return peak, sum_exp, numerator


def iota(shape, dim):
    return lax.broadcasted_iota(jnp.int32, shape, dim)


def head_rows(source, head_group):
    first = 1024 + head_group * 512
    return jnp.concatenate(
        [source[:, first + g * 128 : first + (g + 1) * 128] for g in range(4)], axis=0
    )


def store_partials(target, head_group, partials):
    peak, sum_exp, numerator = partials
    row, lane = iota((32, 128), 0), iota((32, 128), 1)
    for b in range(8):
        part = slice(b * 32, (b + 1) * 32)
        target[head_group * 8 + b, 0:32] = numerator[part]
        stats = jnp.where(lane == row, peak[part], 0.0) + jnp.where(
            lane == row + 32, sum_exp[part], 0.0
        )
        target[head_group * 8 + b, 32:40] = jnp.broadcast_to(
            jnp.sum(stats, axis=0, keepdims=True), (8, 128)
        )


def stat_column(stats, shift):
    row, lane = iota((32, 128), 0), iota((32, 128), 1)
    spread_stats = jnp.broadcast_to(stats, (32, 128))
    return jnp.sum(
        jnp.where(lane == row + shift, spread_stats, 0.0), axis=1, keepdims=True
    )


def layer_kernel(
    context_rows, query_acts, gain, w_query, w_key, value_weight, lengths, block_out, query_out,
    twin_query, twin_key, twin_value, sliced, query_sliced, gathered, partial, first_sum, passed,
    second_sum, query_sums, query_arrived, query_mine, query_parts, context, query,
    anchor, partials, own_partials, received, merged, merged_all,
    twin_send, twin_recv, row_send, row_recv, first_send, first_recv, passed_send, passed_recv,
    second_send, second_recv, query_send, query_recv, spread_send, spread_recv,
    scatter_send, column_send, plane_send, anchor_recv,
    partial_send, partial_recv, merged_send, merged_recv,
):
    outer, inner = lax.axis_index("outer"), lax.axis_index("inner")
    outers, inners = lax.axis_size("outer"), lax.axis_size("inner")
    devices = outers * inners
    me = outer * inners + inner
    chip, core = inner // 2, inner % 2
    twin = chip * 2 + 1 - core

    def peer(step):
        return chip_peer(chip, step)

    def remote(source, target, send, recv, to_outer, to_inner):
        return pltpu.make_async_remote_copy(
            src_ref=source, dst_ref=target, send_sem=send, recv_sem=recv,
            device_id={"outer": to_outer, "inner": to_inner},
            device_id_type=pl.DeviceIdType.MESH,
        )

    barrier = pltpu.get_barrier_semaphore()

    def greet(t, carry):
        other = (me + t) % devices
        pl.semaphore_signal(
            barrier, inc=1, device_id={"outer": other // inners, "inner": other % inners},
            device_id_type=pl.DeviceIdType.MESH,
        )
        return carry

    lax.fori_loop(1, devices, greet, 0)
    @pl.loop(0, context_rows.shape[0] // 16)
    def _(index):
        first = pl.multiple_of(index * 16, 16)
        rows = normalize_rows(context_rows, gain, first, 16)
        for k in range(4):
            sliced[k, pl.ds(first, 16), :] = rows[:, k * 1024 : (k + 1) * 1024]

    pl.semaphore_wait(barrier, devices - 1)

    row_copies = [
        remote(
            sliced.at[peer(step)], gathered.at[step], row_send.at[step], row_recv.at[step],
            outer, peer(step) * 2 + core,
        )
        for step in range(3)
    ]
    for step in (2, 0, 1):
        row_copies[step].start()

    weight_copies = [
        remote(mine, theirs, twin_send.at[k], twin_recv.at[k], outer, twin)
        for k, (mine, theirs) in enumerate(
            ((w_key, twin_key), (value_weight, twin_value), (w_query, twin_query))
        )
    ]
    for copy in weight_copies:
        copy.start()

    @pl.loop(0, query_acts.shape[0] // 16)
    def _(index):
        first = pl.multiple_of(index * 16, 16)
        rows = normalize_rows(query_acts, gain, first, 16)
        for k in range(4):
            query_sliced[k, pl.ds(first, 16), :] = rows[:, k * 1024 : (k + 1) * 1024]

    gathered[3] = sliced[chip]
    for copy in weight_copies:
        copy.wait()

    def tiles(k):
        if k < 2:
            return (w_key, value_weight)[k][...], (twin_key, twin_value)[k][...]
        columns = slice((k - 2) * 512, (k - 1) * 512)
        return w_query[:, columns], twin_query[:, columns]

    own_columns = pl.ds(pl.multiple_of(core * 512, 512), 512)
    twin_columns = pl.ds(pl.multiple_of((1 - core) * 512, 512), 512)

    def product(source, index, k):
        own_tile, twin_tile = tiles(k)
        return jnp.dot(
            source[index, :, own_columns], own_tile, preferred_element_type=jnp.float32
        ) + jnp.dot(
            source[index, :, twin_columns], twin_tile, preferred_element_type=jnp.float32
        )

    for k in range(6):
        query_sums[:, k * 512 : (k + 1) * 512] = product(query_sliced, chip, k)

    def query_part(other):
        return pl.ds(pl.multiple_of(other * 16 + core * 8, 8), 8)

    query_copies = [
        remote(
            query_sums.at[query_part(peer(step))], query_arrived.at[step], query_send.at[step],
            query_recv.at[step], outer, peer(step) * 2 + core,
        )
        for step in range(3)
    ]
    for copy in query_copies:
        copy.start()

    def first_copy(k):
        return remote(
            partial.at[k % 2, k], first_sum.at[k], first_send.at[k], first_recv.at[k],
            outer, peer(k % 2) * 2 + core,
        )

    def passed_copy(k):
        return remote(
            partial.at[2, k], passed.at[k], passed_send.at[k], passed_recv.at[k],
            outer, peer(k % 2) * 2 + core,
        )

    def second_copy(k):
        return remote(
            partial.at[1 - k % 2, k], second_sum.at[k], second_send.at[k], second_recv.at[k],
            outer, peer(1 - k % 2) * 2 + core,
        )

    def multiply(k):
        def one(step, carry):
            partial[step, k] = product(gathered, step, k)
            return carry

        lax.fori_loop(0, 4, one, 0)
        passed_copy(k).start()
        first_copy(k).start()

    def relay(k):
        passed_copy(k).wait()
        partial[1 - k % 2, k] = partial[1 - k % 2, k] + passed[k]
        second_copy(k).start()

    def settle(k):
        first_copy(k).wait()
        second_copy(k).wait()
        total = partial[3, k] + first_sum[k] + second_sum[k]
        context[:, k * 512 : (k + 1) * 512] = total.astype(jnp.bfloat16)

    for step in range(3):
        row_copies[step].wait()
    for k in range(4):
        multiply(k)

    for copy in query_copies:
        copy.wait()
    query_mine[...] = (
        query_sums[query_part(chip), :] + query_arrived[0] + query_arrived[1] + query_arrived[2]
    ).astype(jnp.bfloat16).astype(jnp.float32)

    spread_copies = [
        remote(
            query_mine, query_parts.at[core, chip], spread_send.at[step], spread_recv.at[step],
            outer, peer(step) * 2 + core,
        )
        for step in range(3)
    ]
    for copy in spread_copies:
        copy.start()
    query_parts[core, chip] = query_mine[...]
    relay(0)
    relay(1)
    for k in range(4, 6):
        multiply(k)

    for copy in spread_copies:
        copy.wait()
    twin_copy = remote(
        query_parts.at[core], query_parts.at[core], spread_send.at[3], spread_recv.at[3],
        outer, twin,
    )
    twin_copy.start()
    relay(2)
    relay(3)
    twin_copy.wait()
    for pair in range(4):
        query[pair * 16 : (pair + 1) * 16] = jnp.concatenate(
            [query_parts[0, pair], query_parts[1, pair]], axis=0
        ).astype(jnp.bfloat16)
    settle(0)
    settle(1)

    def scatter_copy(j):
        return remote(
            context.at[:, pl.ds(j * 128, 128)], anchor.at[j], scatter_send.at[j],
            anchor_recv.at[j], 0, j,
        )

    @pl.when(me == 0)
    def _():
        for j in range(1, 8):
            scatter_copy(j).start()
        anchor[0] = context[:, 0:128]

    own_length, anchor_length = lengths[me], lengths[0]

    for h in range(4):
        keys = context[:, h * 128 : (h + 1) * 128]
        values = context[:, 512 + h * 128 : 512 + (h + 1) * 128]
        reached = iota((256, 128), 1) < own_length
        store_partials(partials, h, masked_softmax(head_rows(query, h), keys, values, reached))

    def partial_copy(other):
        return lambda slot: remote(
            partials.at[other], received.at[slot], partial_send.at[other], partial_recv.at[slot],
            other // inners, other % inners,
        )

    def send_partial(t, carry):
        partial_copy((me + t) % devices)(me).start()
        return carry

    lax.fori_loop(1, devices, send_partial, 0)

    relay(4)
    relay(5)

    def column_copy(o):
        return remote(
            anchor.at[inner], anchor.at[inner], column_send.at[o], anchor_recv.at[inner], o, inner
        )

    def plane_copy(j, slot):
        return remote(
            anchor.at[slot], anchor.at[slot], plane_send.at[j], anchor_recv.at[slot], outer, j
        )

    @pl.when(me != 0)
    def _():
        plane_copy(inner, inner).wait_recv()

    @pl.when(outer == 0)
    def _():
        for o in range(1, 4):
            column_copy(o).start()

    def send_plane(t, carry):
        plane_copy((inner + t) % inners, inner).start()
        return carry

    lax.fori_loop(1, inners, send_plane, 0)

    for h in range(4):
        keys = query[:, h * 128 : (h + 1) * 128]
        values = query[:, 512 + h * 128 : 512 + (h + 1) * 128]
        causal = iota((256, 64), 0) % 64 >= iota((256, 64), 1)
        store_partials(own_partials, h, masked_softmax(head_rows(query, h), keys, values, causal))
    received[me] = partials[me]
    received[devices] = own_partials[me]

    def wait_partial(t, carry):
        other = (me + t) % devices
        partial_copy(other)(other).wait()
        return carry

    lax.fori_loop(1, devices, wait_partial, 0)

    def highest(s, peak):
        return jnp.maximum(peak, stat_column(received[s, 32:33], 0))

    top = lax.fori_loop(
        0, devices + 1, highest, jnp.full((32, 1), -jnp.inf, jnp.float32)
    )

    def add_up(s, carry):
        total, numerator = carry
        factor = jnp.exp(stat_column(received[s, 32:33], 0) - top)
        return (
            total + stat_column(received[s, 32:33], 32) * factor,
            numerator + received[s, 0:32] * factor,
        )

    total, numerator = lax.fori_loop(
        0, devices + 1, add_up,
        (jnp.zeros((32, 1), jnp.float32), jnp.zeros((32, 128), jnp.float32)),
    )
    merged[...] = (numerator / total).astype(jnp.bfloat16)

    def merged_copy(other, slot):
        return remote(
            merged, merged_all.at[slot], merged_send.at[other], merged_recv.at[slot],
            other // inners, other % inners,
        )

    def send_merged(t, carry):
        merged_copy((me + t) % devices, me).start()
        return carry

    lax.fori_loop(1, devices, send_merged, 0)
    merged_all[me] = merged[...]

    def wait_plane(t, carry):
        other = (inner + t) % inners
        plane_copy(other, inner).wait_send()
        plane_copy(other, other).wait_recv()
        return carry

    lax.fori_loop(1, inners, wait_plane, 0)

    row, column = iota((512, 256), 0) % 128, iota((512, 256), 1)
    place = column % 128
    limit = jnp.where(column < 128, jnp.where(me > 0, anchor_length, 0), own_length)
    allowed = (place < limit) & ((column < 128) | (row >= place))
    for h in range(4):
        settle(2 + h)
        keys = jnp.concatenate([anchor[h], context[:, h * 128 : (h + 1) * 128]], axis=0)
        values = jnp.concatenate(
            [anchor[4 + h], context[:, 512 + h * 128 : 512 + (h + 1) * 128]], axis=0
        )
        _, sum_exp, numerator = masked_softmax(head_rows(context, h), keys, values, allowed)
        result = (numerator / sum_exp).astype(jnp.bfloat16)
        for g in range(4):
            block_out[:, (h * 4 + g) * 128 : (h * 4 + g + 1) * 128] = result[
                g * 128 : (g + 1) * 128
            ]

    @pl.when(me == 0)
    def _():
        for j in range(1, 8):
            scatter_copy(j).wait_send()

    @pl.when(outer == 0)
    def _():
        for o in range(1, 4):
            column_copy(o).wait_send()

    def wait_merged(t, carry):
        other = (me + t) % devices
        merged_copy(other, other).wait()
        return carry

    lax.fori_loop(1, devices, wait_merged, 0)
    for d in range(32):
        query_out[d % 2 * 32 : d % 2 * 32 + 32, d // 2 * 128 : d // 2 * 128 + 128] = merged_all[d]


def layer(context, query_acts, norm_gain, w_query, w_key, value_weight, lengths):
    vmem = pl.BlockSpec(memory_space=pltpu.VMEM)
    bf16, f32, dma = jnp.bfloat16, jnp.float32, pltpu.SemaphoreType.DMA
    buffers = [
        ((512, 2048), bf16), ((512, 512), bf16), ((512, 512), bf16),
        ((4, 128, 1024), bf16), ((4, 64, 1024), bf16), ((4, 128, 1024), bf16),
        ((4, 6, 128, 512), f32), ((6, 128, 512), f32), ((6, 128, 512), f32),
        ((6, 128, 512), f32), ((64, 3072), f32), ((3, 8, 3072), f32), ((8, 3072), f32),
        ((2, 4, 8, 3072), f32), ((128, 3072), bf16), ((64, 3072), bf16),
        ((8, 128, 128), bf16), ((32, 40, 128), f32), ((32, 40, 128), f32),
        ((33, 40, 128), f32), ((32, 128), bf16), ((32, 32, 128), bf16),
    ]
    counts = [3, 3, 3, 3, 6, 6, 6, 6, 6, 6, 3, 3, 8, 8, 8, 4, 8, 8, 32, 32, 32, 32]
    return pl.pallas_call(
        layer_kernel,
        out_shape=[
            jax.ShapeDtypeStruct((128, 2048), bf16),
            jax.ShapeDtypeStruct((64, 2048), bf16),
        ],
        in_specs=[vmem] * 6 + [pl.BlockSpec(memory_space=pltpu.SMEM)],
        out_specs=[vmem] * 2,
        scratch_shapes=[pltpu.VMEM(shape, kind) for shape, kind in buffers]
        + [dma((count,)) for count in counts],
        compiler_params=pltpu.CompilerParams(
            collective_id=0, has_side_effects=True, vmem_limit_bytes=40 * 2**20
        ),
        cost_estimate=pl.CostEstimate(
            flops=5 * 10**9, bytes_accessed=8 * 2**20, transcendentals=10**6
        ),
    )(context, query_acts, norm_gain.reshape(1, -1), w_query, w_key, value_weight, lengths)


def attend_part(query_rows, key_row_block, value_matrix, allowed):
    count_of_rows = query_rows.shape[0]
    head_groups = query_rows.reshape(
        count_of_rows, KEY_VALUE_HEADS, QUERY_HEADS // KEY_VALUE_HEADS, HEAD_SIZE
    )
    per_head_keys = key_row_block.reshape(key_row_block.shape[0], KEY_VALUE_HEADS, HEAD_SIZE)
    per_head_values = value_matrix.reshape(value_matrix.shape[0], KEY_VALUE_HEADS, HEAD_SIZE)
    scores = jnp.einsum(
        "rhgd,khd->hgrk", head_groups, per_head_keys, preferred_element_type=jnp.float32
    ) * HEAD_SIZE ** (-0.5)
    scores = jnp.where(allowed, scores, -jnp.inf)
    maxima = jnp.max(scores, axis=-1)
    weights = jnp.exp(scores - maxima[..., None])
    sum_exp = jnp.sum(weights, axis=-1)
    numerator = jnp.einsum(
        "hgrk,khd->rhgd",
        weights.astype(jnp.bfloat16),
        per_head_values,
        preferred_element_type=jnp.float32,
    )
    return (
        maxima.reshape(QUERY_HEADS, count_of_rows),
        sum_exp.reshape(QUERY_HEADS, count_of_rows),
        numerator.reshape(count_of_rows, QUERY_HEADS * HEAD_SIZE),
    )


def spread(factor):
    return jnp.repeat(factor.T, HEAD_SIZE, axis=1)


def combine(former, latter):
    maxima = jnp.maximum(former[0], latter[0])
    scale_one = jnp.exp(former[0] - maxima)
    scale_two = jnp.exp(latter[0] - maxima)
    return (
        maxima,
        former[1] * scale_one + latter[1] * scale_two,
        former[2] * spread(scale_one) + latter[2] * spread(scale_two),
    )


def finish(pieces):
    return (pieces[2] / spread(pieces[1])).astype(jnp.bfloat16)


def share_anchor(stacked):
    return broadcast(stacked, ("outer", "inner"), 0)


def project_all(context, query_acts, norm_gain, w_query, w_key, value_weight):
    normed = jnp.concatenate(
        [normalize(context, norm_gain), normalize(query_acts, norm_gain)], axis=0
    )
    return tuple(
        jnp.dot(
            normed,
            lax.all_gather(weight, "inner", axis=0, tiled=True),
            preferred_element_type=jnp.float32,
        ).astype(jnp.bfloat16)
        for weight in (w_query, w_key, value_weight)
    )


def per_device(context, query_acts, norm_gain, w_query, w_key, value_weight, lengths):
    if (lax.axis_size("outer"), lax.axis_size("inner")) == (4, 8):
        return tuple(
            layer(context, query_acts, norm_gain, w_query, w_key, value_weight, lengths)
        )
    block_rows = context.shape[0]
    projected_q, projected_k, projected_v = project_all(
        context, query_acts, norm_gain, w_query, w_key, value_weight
    )
    anchor = share_anchor(jnp.stack([projected_k[:block_rows], projected_v[:block_rows]]))
    position = lax.axis_index(("outer", "inner"))
    own_length = lengths[position]
    anchor_length = lengths[0]
    places = jnp.arange(block_rows, dtype=jnp.int32)
    causal = places[:, None] >= places[None, :]
    block_q = projected_q[:block_rows]
    block_k = projected_k[:block_rows]
    block_v = projected_v[:block_rows]
    query_q = projected_q[block_rows:]
    query_k = projected_k[block_rows:]
    query_v = projected_v[block_rows:]
    query_count = query_q.shape[0]
    own_allowed = causal & (places[None, :] < own_length)
    anchor_allowed = jnp.broadcast_to(
        (places[None, :] < anchor_length) & (position > 0), (block_rows, block_rows)
    )
    allowed = jnp.concatenate([anchor_allowed, own_allowed], axis=1)
    key_row_block = jnp.concatenate([anchor[0], block_k], axis=0)
    value_rows = jnp.concatenate([anchor[1], block_v], axis=0)
    block_out = finish(attend_part(block_q, key_row_block, value_rows, allowed))
    reached = jnp.broadcast_to(places[None, :] < own_length, (query_count, block_rows))
    block_part = attend_part(query_q, block_k, block_v, reached)
    highest = lax.pmax(block_part[0], ("outer", "inner"))
    rescale = jnp.exp(block_part[0] - highest)
    summed_parts = lax.psum(
        (block_part[1] * rescale, block_part[2] * spread(rescale)), ("outer", "inner")
    )
    merged = (highest, summed_parts[0], summed_parts[1])
    query_places = jnp.arange(query_count, dtype=jnp.int32)
    self_part = attend_part(
        query_q, query_k, query_v, query_places[:, None] >= query_places[None, :]
    )
    return (block_out, finish(combine(merged, self_part)))


def solution(mesh):
    in_specs = (
        P(("outer", "inner"), None),
        P(),
        P(),
        P("inner", None),
        P("inner", None),
        P("inner", None),
        P(),
    )
    out_specs = (P(("outer", "inner"), None), P())
    return jax.shard_map(
        per_device, mesh=mesh, in_specs=in_specs, out_specs=out_specs, check_vma=False
    )
```

```python
import jax
import jax.numpy as jnp
from jax import lax
from jax.experimental import pallas as pl
from jax.experimental.pallas import tpu as pltpu
from jax.sharding import PartitionSpec as P

QUERY_HEADS = 16
KEY_VALUE_HEADS = 4
HEAD_SIZE = 128


epsilon = 1e-05


def broadcast(block, axis, owner):
    block = jnp.where(lax.axis_index(axis) == owner, block, jnp.zeros_like(block))
    return lax.psum(block, axis)


def normalize(matrix, norm_gain):
    widened = matrix.astype(jnp.float32)
    factor = lax.rsqrt(jnp.mean(widened * widened, axis=-1, keepdims=True) + epsilon)
    return (widened * factor * norm_gain).astype(jnp.bfloat16)


def chip_peer(chip, step):
    offset = (step + 1) % 4
    return (chip // 2 + offset // 2) % 2 * 2 + (chip + offset) % 2


def normalize_rows(source, gain, first, count):
    widened = source[pl.ds(first, count), :].astype(jnp.float32)
    factor = lax.rsqrt(jnp.mean(widened * widened, axis=-1, keepdims=True) + epsilon)
    return (widened * factor * gain[...]).astype(jnp.bfloat16)


def masked_softmax(rows, keys, values, allowed):
    scores = lax.dot_general(
        rows, keys, (((1,), (1,)), ((), ())), preferred_element_type=jnp.float32
    ) * HEAD_SIZE ** (-0.5)
    scores = jnp.where(allowed, scores, -jnp.inf)
    peak = jnp.max(scores, axis=-1, keepdims=True)
    weights = jnp.exp(scores - peak)
    sum_exp = jnp.sum(weights, axis=-1, keepdims=True)
    numerator = jnp.dot(
        weights.astype(jnp.bfloat16), values, preferred_element_type=jnp.float32
    )
    return peak, sum_exp, numerator


def iota(shape, dim):
    return lax.broadcasted_iota(jnp.int32, shape, dim)


def head_rows(source, head_group):
    first = 1024 + head_group * 512
    return jnp.concatenate(
        [source[:, first + g * 128 : first + (g + 1) * 128] for g in range(4)], axis=0
    )


def store_partials(target, head_group, partials):
    peak, sum_exp, numerator = partials
    row, lane = iota((32, 128), 0), iota((32, 128), 1)
    for b in range(8):
        part = slice(b * 32, (b + 1) * 32)
        target[head_group * 8 + b, 0:32] = numerator[part]
        stats = jnp.where(lane == row, peak[part], 0.0) + jnp.where(
            lane == row + 32, sum_exp[part], 0.0
        )
        target[head_group * 8 + b, 32:40] = jnp.broadcast_to(
            jnp.sum(stats, axis=0, keepdims=True), (8, 128)
        )


def stat_column(stats, shift):
    row, lane = iota((32, 128), 0), iota((32, 128), 1)
    spread_stats = jnp.broadcast_to(stats, (32, 128))
    return jnp.sum(
        jnp.where(lane == row + shift, spread_stats, 0.0), axis=1, keepdims=True
    )


def layer_kernel(
    context_far, query_far, gain_far, w_query_far, w_key_far, value_far, lengths, block_out, query_out,
    context_rows, query_acts, gain, w_query, w_key, value_weight, load_sem,
    twin_query, twin_key, twin_value, sliced, query_sliced, gathered, partial, first_sum, passed,
    second_sum, query_sums, query_arrived, query_mine, query_parts, context, query,
    anchor, partials, own_partials, received, merged, merged_all,
    twin_send, twin_recv, row_send, row_recv, first_send, first_recv, passed_send, passed_recv,
    second_send, second_recv, query_send, query_recv, spread_send, spread_recv,
    scatter_send, column_send, plane_send, anchor_recv,
    partial_send, partial_recv, merged_send, merged_recv,
):
    outer, inner = lax.axis_index("outer"), lax.axis_index("inner")
    outers, inners = lax.axis_size("outer"), lax.axis_size("inner")
    devices = outers * inners
    me = outer * inners + inner
    loads = [
        pltpu.make_async_copy(far, near, load_sem.at[k])
        for k, (far, near) in enumerate(
            (
                (gain_far, gain), (context_far, context_rows), (w_key_far, w_key),
                (value_far, value_weight), (w_query_far, w_query), (query_far, query_acts),
            )
        )
    ]
    for load in loads:
        load.start()
    chip, core = inner // 2, inner % 2
    twin = chip * 2 + 1 - core

    def peer(step):
        return chip_peer(chip, step)

    def remote(source, target, send, recv, to_outer, to_inner):
        return pltpu.make_async_remote_copy(
            src_ref=source, dst_ref=target, send_sem=send, recv_sem=recv,
            device_id={"outer": to_outer, "inner": to_inner},
            device_id_type=pl.DeviceIdType.MESH,
        )

    barrier = pltpu.get_barrier_semaphore()

    def greet(t, carry):
        other = (me + t) % devices
        pl.semaphore_signal(
            barrier, inc=1, device_id={"outer": other // inners, "inner": other % inners},
            device_id_type=pl.DeviceIdType.MESH,
        )
        return carry

    lax.fori_loop(1, devices, greet, 0)
    loads[0].wait()
    loads[1].wait()

    @pl.loop(0, context_rows.shape[0] // 16)
    def _(index):
        first = pl.multiple_of(index * 16, 16)
        rows = normalize_rows(context_rows, gain, first, 16)
        for k in range(4):
            sliced[k, pl.ds(first, 16), :] = rows[:, k * 1024 : (k + 1) * 1024]

    pl.semaphore_wait(barrier, devices - 1)

    row_copies = [
        remote(
            sliced.at[peer(step)], gathered.at[step], row_send.at[step], row_recv.at[step],
            outer, peer(step) * 2 + core,
        )
        for step in range(3)
    ]
    for step in (2, 0, 1):
        row_copies[step].start()

    for load in loads[2:]:
        load.wait()
    weight_copies = [
        remote(mine, theirs, twin_send.at[k], twin_recv.at[k], outer, twin)
        for k, (mine, theirs) in enumerate(
            ((w_key, twin_key), (value_weight, twin_value), (w_query, twin_query))
        )
    ]
    for copy in weight_copies:
        copy.start()

    @pl.loop(0, query_acts.shape[0] // 16)
    def _(index):
        first = pl.multiple_of(index * 16, 16)
        rows = normalize_rows(query_acts, gain, first, 16)
        for k in range(4):
            query_sliced[k, pl.ds(first, 16), :] = rows[:, k * 1024 : (k + 1) * 1024]

    gathered[3] = sliced[chip]
    for copy in weight_copies:
        copy.wait()

    def tiles(k):
        if k < 2:
            return (w_key, value_weight)[k][...], (twin_key, twin_value)[k][...]
        columns = slice((k - 2) * 512, (k - 1) * 512)
        return w_query[:, columns], twin_query[:, columns]

    own_columns = pl.ds(pl.multiple_of(core * 512, 512), 512)
    twin_columns = pl.ds(pl.multiple_of((1 - core) * 512, 512), 512)

    def product(source, index, k):
        own_tile, twin_tile = tiles(k)
        return jnp.dot(
            source[index, :, own_columns], own_tile, preferred_element_type=jnp.float32
        ) + jnp.dot(
            source[index, :, twin_columns], twin_tile, preferred_element_type=jnp.float32
        )

    for k in range(6):
        query_sums[:, k * 512 : (k + 1) * 512] = product(query_sliced, chip, k)

    def query_part(other):
        return pl.ds(pl.multiple_of(other * 16 + core * 8, 8), 8)

    query_copies = [
        remote(
            query_sums.at[query_part(peer(step))], query_arrived.at[step], query_send.at[step],
            query_recv.at[step], outer, peer(step) * 2 + core,
        )
        for step in range(3)
    ]
    for copy in query_copies:
        copy.start()

    def first_copy(k):
        return remote(
            partial.at[k % 2, k], first_sum.at[k], first_send.at[k], first_recv.at[k],
            outer, peer(k % 2) * 2 + core,
        )

    def passed_copy(k):
        return remote(
            partial.at[2, k], passed.at[k], passed_send.at[k], passed_recv.at[k],
            outer, peer(k % 2) * 2 + core,
        )

    def second_copy(k):
        return remote(
            partial.at[1 - k % 2, k], second_sum.at[k], second_send.at[k], second_recv.at[k],
            outer, peer(1 - k % 2) * 2 + core,
        )

    def multiply(k):
        def one(step, carry):
            partial[step, k] = product(gathered, step, k)
            return carry

        lax.fori_loop(0, 4, one, 0)
        passed_copy(k).start()
        first_copy(k).start()

    def relay(k):
        passed_copy(k).wait()
        partial[1 - k % 2, k] = partial[1 - k % 2, k] + passed[k]
        second_copy(k).start()

    def settle(k):
        first_copy(k).wait()
        second_copy(k).wait()
        total = partial[3, k] + first_sum[k] + second_sum[k]
        context[:, k * 512 : (k + 1) * 512] = total.astype(jnp.bfloat16)

    for step in range(3):
        row_copies[step].wait()
    for k in range(4):
        multiply(k)

    for copy in query_copies:
        copy.wait()
    query_mine[...] = (
        query_sums[query_part(chip), :] + query_arrived[0] + query_arrived[1] + query_arrived[2]
    ).astype(jnp.bfloat16).astype(jnp.float32)

    spread_copies = [
        remote(
            query_mine, query_parts.at[core, chip], spread_send.at[step], spread_recv.at[step],
            outer, peer(step) * 2 + core,
        )
        for step in range(3)
    ]
    for copy in spread_copies:
        copy.start()
    query_parts[core, chip] = query_mine[...]
    relay(0)
    relay(1)
    for k in range(4, 6):
        multiply(k)

    for copy in spread_copies:
        copy.wait()
    twin_copy = remote(
        query_parts.at[core], query_parts.at[core], spread_send.at[3], spread_recv.at[3],
        outer, twin,
    )
    twin_copy.start()
    relay(2)
    relay(3)
    twin_copy.wait()
    for pair in range(4):
        query[pair * 16 : (pair + 1) * 16] = jnp.concatenate(
            [query_parts[0, pair], query_parts[1, pair]], axis=0
        ).astype(jnp.bfloat16)
    settle(0)
    settle(1)

    def scatter_copy(j):
        return remote(
            context.at[:, pl.ds(j * 128, 128)], anchor.at[j], scatter_send.at[j],
            anchor_recv.at[j], 0, j,
        )

    @pl.when(me == 0)
    def _():
        for j in range(1, 8):
            scatter_copy(j).start()
        anchor[0] = context[:, 0:128]

    own_length, anchor_length = lengths[me], lengths[0]

    for h in range(4):
        keys = context[:, h * 128 : (h + 1) * 128]
        values = context[:, 512 + h * 128 : 512 + (h + 1) * 128]
        reached = iota((256, 128), 1) < own_length
        store_partials(partials, h, masked_softmax(head_rows(query, h), keys, values, reached))

    def partial_copy(other):
        return lambda slot: remote(
            partials.at[other], received.at[slot], partial_send.at[other], partial_recv.at[slot],
            other // inners, other % inners,
        )

    def send_partial(t, carry):
        partial_copy((me + t) % devices)(me).start()
        return carry

    lax.fori_loop(1, devices, send_partial, 0)

    relay(4)
    relay(5)

    def column_copy(o):
        return remote(
            anchor.at[inner], anchor.at[inner], column_send.at[o], anchor_recv.at[inner], o, inner
        )

    def plane_copy(j, slot):
        return remote(
            anchor.at[slot], anchor.at[slot], plane_send.at[j], anchor_recv.at[slot], outer, j
        )

    @pl.when(me != 0)
    def _():
        plane_copy(inner, inner).wait_recv()

    @pl.when(outer == 0)
    def _():
        for o in range(1, 4):
            column_copy(o).start()

    def send_plane(t, carry):
        plane_copy((inner + t) % inners, inner).start()
        return carry

    lax.fori_loop(1, inners, send_plane, 0)

    for h in range(4):
        keys = query[:, h * 128 : (h + 1) * 128]
        values = query[:, 512 + h * 128 : 512 + (h + 1) * 128]
        causal = iota((256, 64), 0) % 64 >= iota((256, 64), 1)
        store_partials(own_partials, h, masked_softmax(head_rows(query, h), keys, values, causal))
    received[me] = partials[me]
    received[devices] = own_partials[me]

    def wait_partial(t, carry):
        other = (me + t) % devices
        partial_copy(other)(other).wait()
        return carry

    lax.fori_loop(1, devices, wait_partial, 0)

    def highest(s, peak):
        return jnp.maximum(peak, stat_column(received[s, 32:33], 0))

    top = lax.fori_loop(
        0, devices + 1, highest, jnp.full((32, 1), -jnp.inf, jnp.float32)
    )

    def add_up(s, carry):
        total, numerator = carry
        factor = jnp.exp(stat_column(received[s, 32:33], 0) - top)
        return (
            total + stat_column(received[s, 32:33], 32) * factor,
            numerator + received[s, 0:32] * factor,
        )

    total, numerator = lax.fori_loop(
        0, devices + 1, add_up,
        (jnp.zeros((32, 1), jnp.float32), jnp.zeros((32, 128), jnp.float32)),
    )
    merged[...] = (numerator / total).astype(jnp.bfloat16)

    def merged_copy(other, slot):
        return remote(
            merged, merged_all.at[slot], merged_send.at[other], merged_recv.at[slot],
            other // inners, other % inners,
        )

    def send_merged(t, carry):
        merged_copy((me + t) % devices, me).start()
        return carry

    lax.fori_loop(1, devices, send_merged, 0)
    merged_all[me] = merged[...]

    def wait_plane(t, carry):
        other = (inner + t) % inners
        plane_copy(other, inner).wait_send()
        plane_copy(other, other).wait_recv()
        return carry

    lax.fori_loop(1, inners, wait_plane, 0)

    row, column = iota((512, 256), 0) % 128, iota((512, 256), 1)
    place = column % 128
    limit = jnp.where(column < 128, jnp.where(me > 0, anchor_length, 0), own_length)
    allowed = (place < limit) & ((column < 128) | (row >= place))
    for h in range(4):
        settle(2 + h)
        keys = jnp.concatenate([anchor[h], context[:, h * 128 : (h + 1) * 128]], axis=0)
        values = jnp.concatenate(
            [anchor[4 + h], context[:, 512 + h * 128 : 512 + (h + 1) * 128]], axis=0
        )
        _, sum_exp, numerator = masked_softmax(head_rows(context, h), keys, values, allowed)
        result = (numerator / sum_exp).astype(jnp.bfloat16)
        for g in range(4):
            block_out[:, (h * 4 + g) * 128 : (h * 4 + g + 1) * 128] = result[
                g * 128 : (g + 1) * 128
            ]

    @pl.when(me == 0)
    def _():
        for j in range(1, 8):
            scatter_copy(j).wait_send()

    @pl.when(outer == 0)
    def _():
        for o in range(1, 4):
            column_copy(o).wait_send()

    def wait_merged(t, carry):
        other = (me + t) % devices
        merged_copy(other, other).wait()
        return carry

    lax.fori_loop(1, devices, wait_merged, 0)
    for d in range(32):
        query_out[d % 2 * 32 : d % 2 * 32 + 32, d // 2 * 128 : d // 2 * 128 + 128] = merged_all[d]


def layer(context, query_acts, norm_gain, w_query, w_key, value_weight, lengths):
    vmem = pl.BlockSpec(memory_space=pltpu.VMEM)
    bf16, f32, dma = jnp.bfloat16, jnp.float32, pltpu.SemaphoreType.DMA
    buffers = [
        ((512, 2048), bf16), ((512, 512), bf16), ((512, 512), bf16),
        ((4, 128, 1024), bf16), ((4, 64, 1024), bf16), ((4, 128, 1024), bf16),
        ((4, 6, 128, 512), f32), ((6, 128, 512), f32), ((6, 128, 512), f32),
        ((6, 128, 512), f32), ((64, 3072), f32), ((3, 8, 3072), f32), ((8, 3072), f32),
        ((2, 4, 8, 3072), f32), ((128, 3072), bf16), ((64, 3072), bf16),
        ((8, 128, 128), bf16), ((32, 40, 128), f32), ((32, 40, 128), f32),
        ((33, 40, 128), f32), ((32, 128), bf16), ((32, 32, 128), bf16),
    ]
    counts = [3, 3, 3, 3, 6, 6, 6, 6, 6, 6, 3, 3, 8, 8, 8, 4, 8, 8, 32, 32, 32, 32]
    return pl.pallas_call(
        layer_kernel,
        out_shape=[
            jax.ShapeDtypeStruct((128, 2048), bf16),
            jax.ShapeDtypeStruct((64, 2048), bf16),
        ],
        in_specs=[pl.BlockSpec(memory_space=pltpu.HBM)] * 6
        + [pl.BlockSpec(memory_space=pltpu.SMEM)],
        out_specs=[vmem] * 2,
        scratch_shapes=[
            pltpu.VMEM((128, 4096), bf16), pltpu.VMEM((64, 4096), bf16), pltpu.VMEM((1, 4096), f32),
            pltpu.VMEM((512, 2048), bf16), pltpu.VMEM((512, 512), bf16),
            pltpu.VMEM((512, 512), bf16), dma((6,)),
        ]
        + [pltpu.VMEM(shape, kind) for shape, kind in buffers]
        + [dma((count,)) for count in counts],
        compiler_params=pltpu.CompilerParams(
            collective_id=0, has_side_effects=True, vmem_limit_bytes=56 * 2**20
        ),
        cost_estimate=pl.CostEstimate(
            flops=5 * 10**9, bytes_accessed=8 * 2**20, transcendentals=10**6
        ),
    )(context, query_acts, norm_gain.reshape(1, -1), w_query, w_key, value_weight, lengths)


def attend_part(query_rows, key_row_block, value_matrix, allowed):
    count_of_rows = query_rows.shape[0]
    head_groups = query_rows.reshape(
        count_of_rows, KEY_VALUE_HEADS, QUERY_HEADS // KEY_VALUE_HEADS, HEAD_SIZE
    )
    per_head_keys = key_row_block.reshape(key_row_block.shape[0], KEY_VALUE_HEADS, HEAD_SIZE)
    per_head_values = value_matrix.reshape(value_matrix.shape[0], KEY_VALUE_HEADS, HEAD_SIZE)
    scores = jnp.einsum(
        "rhgd,khd->hgrk", head_groups, per_head_keys, preferred_element_type=jnp.float32
    ) * HEAD_SIZE ** (-0.5)
    scores = jnp.where(allowed, scores, -jnp.inf)
    maxima = jnp.max(scores, axis=-1)
    weights = jnp.exp(scores - maxima[..., None])
    sum_exp = jnp.sum(weights, axis=-1)
    numerator = jnp.einsum(
        "hgrk,khd->rhgd",
        weights.astype(jnp.bfloat16),
        per_head_values,
        preferred_element_type=jnp.float32,
    )
    return (
        maxima.reshape(QUERY_HEADS, count_of_rows),
        sum_exp.reshape(QUERY_HEADS, count_of_rows),
        numerator.reshape(count_of_rows, QUERY_HEADS * HEAD_SIZE),
    )


def spread(factor):
    return jnp.repeat(factor.T, HEAD_SIZE, axis=1)


def combine(former, latter):
    maxima = jnp.maximum(former[0], latter[0])
    scale_one = jnp.exp(former[0] - maxima)
    scale_two = jnp.exp(latter[0] - maxima)
    return (
        maxima,
        former[1] * scale_one + latter[1] * scale_two,
        former[2] * spread(scale_one) + latter[2] * spread(scale_two),
    )


def finish(pieces):
    return (pieces[2] / spread(pieces[1])).astype(jnp.bfloat16)


def share_anchor(stacked):
    return broadcast(stacked, ("outer", "inner"), 0)


def project_all(context, query_acts, norm_gain, w_query, w_key, value_weight):
    normed = jnp.concatenate(
        [normalize(context, norm_gain), normalize(query_acts, norm_gain)], axis=0
    )
    return tuple(
        jnp.dot(
            normed,
            lax.all_gather(weight, "inner", axis=0, tiled=True),
            preferred_element_type=jnp.float32,
        ).astype(jnp.bfloat16)
        for weight in (w_query, w_key, value_weight)
    )


def per_device(context, query_acts, norm_gain, w_query, w_key, value_weight, lengths):
    if (lax.axis_size("outer"), lax.axis_size("inner")) == (4, 8):
        return tuple(
            layer(context, query_acts, norm_gain, w_query, w_key, value_weight, lengths)
        )
    block_rows = context.shape[0]
    projected_q, projected_k, projected_v = project_all(
        context, query_acts, norm_gain, w_query, w_key, value_weight
    )
    anchor = share_anchor(jnp.stack([projected_k[:block_rows], projected_v[:block_rows]]))
    position = lax.axis_index(("outer", "inner"))
    own_length = lengths[position]
    anchor_length = lengths[0]
    places = jnp.arange(block_rows, dtype=jnp.int32)
    causal = places[:, None] >= places[None, :]
    block_q = projected_q[:block_rows]
    block_k = projected_k[:block_rows]
    block_v = projected_v[:block_rows]
    query_q = projected_q[block_rows:]
    query_k = projected_k[block_rows:]
    query_v = projected_v[block_rows:]
    query_count = query_q.shape[0]
    own_allowed = causal & (places[None, :] < own_length)
    anchor_allowed = jnp.broadcast_to(
        (places[None, :] < anchor_length) & (position > 0), (block_rows, block_rows)
    )
    allowed = jnp.concatenate([anchor_allowed, own_allowed], axis=1)
    key_row_block = jnp.concatenate([anchor[0], block_k], axis=0)
    value_rows = jnp.concatenate([anchor[1], block_v], axis=0)
    block_out = finish(attend_part(block_q, key_row_block, value_rows, allowed))
    reached = jnp.broadcast_to(places[None, :] < own_length, (query_count, block_rows))
    block_part = attend_part(query_q, block_k, block_v, reached)
    highest = lax.pmax(block_part[0], ("outer", "inner"))
    rescale = jnp.exp(block_part[0] - highest)
    summed_parts = lax.psum(
        (block_part[1] * rescale, block_part[2] * spread(rescale)), ("outer", "inner")
    )
    merged = (highest, summed_parts[0], summed_parts[1])
    query_places = jnp.arange(query_count, dtype=jnp.int32)
    self_part = attend_part(
        query_q, query_k, query_v, query_places[:, None] >= query_places[None, :]
    )
    return (block_out, finish(combine(merged, self_part)))


def solution(mesh):
    in_specs = (
        P(("outer", "inner"), None),
        P(),
        P(),
        P("inner", None),
        P("inner", None),
        P("inner", None),
        P(),
    )
    out_specs = (P(("outer", "inner"), None), P())
    return jax.shard_map(
        per_device, mesh=mesh, in_specs=in_specs, out_specs=out_specs, check_vma=False
    )
```

```python
import jax
import jax.numpy as jnp
from jax import lax
from jax.experimental import pallas as pl
from jax.experimental.pallas import tpu as pltpu
from jax.sharding import PartitionSpec as P

QUERY_HEADS = 16
KEY_VALUE_HEADS = 4
HEAD_SIZE = 128


epsilon = 1e-05


def broadcast(block, axis, owner):
    block = jnp.where(lax.axis_index(axis) == owner, block, jnp.zeros_like(block))
    return lax.psum(block, axis)


def normalize(matrix, norm_gain):
    widened = matrix.astype(jnp.float32)
    factor = lax.rsqrt(jnp.mean(widened * widened, axis=-1, keepdims=True) + epsilon)
    return (widened * factor * norm_gain).astype(jnp.bfloat16)


def chip_peer(chip, step):
    offset = (step + 1) % 4
    return (chip // 2 + offset // 2) % 2 * 2 + (chip + offset) % 2


def normalize_rows(source, gain, first, count):
    widened = source[pl.ds(first, count), :].astype(jnp.float32)
    factor = lax.rsqrt(jnp.mean(widened * widened, axis=-1, keepdims=True) + epsilon)
    return (widened * factor * gain[...]).astype(jnp.bfloat16)


def masked_softmax(rows, keys, values, allowed):
    scores = lax.dot_general(
        rows, keys, (((1,), (1,)), ((), ())), preferred_element_type=jnp.float32
    ) * HEAD_SIZE ** (-0.5)
    scores = jnp.where(allowed, scores, -jnp.inf)
    peak = jnp.max(scores, axis=-1, keepdims=True)
    weights = jnp.exp(scores - peak)
    sum_exp = jnp.sum(weights, axis=-1, keepdims=True)
    numerator = jnp.dot(
        weights.astype(jnp.bfloat16), values, preferred_element_type=jnp.float32
    )
    return peak, sum_exp, numerator


def iota(shape, dim):
    return lax.broadcasted_iota(jnp.int32, shape, dim)


def head_rows(source, head_group):
    first = 1024 + head_group * 512
    return jnp.concatenate(
        [source[:, first + g * 128 : first + (g + 1) * 128] for g in range(4)], axis=0
    )


def store_partials(target, head_group, partials):
    peak, sum_exp, numerator = partials
    row, lane = iota((32, 128), 0), iota((32, 128), 1)
    for b in range(8):
        part = slice(b * 32, (b + 1) * 32)
        target[head_group * 8 + b, 0:32] = numerator[part]
        stats = jnp.where(lane == row, peak[part], 0.0) + jnp.where(
            lane == row + 32, sum_exp[part], 0.0
        )
        target[head_group * 8 + b, 32:40] = jnp.broadcast_to(
            jnp.sum(stats, axis=0, keepdims=True), (8, 128)
        )


def stat_column(stats, shift):
    row, lane = iota((32, 128), 0), iota((32, 128), 1)
    spread_stats = jnp.broadcast_to(stats, (32, 128))
    return jnp.sum(
        jnp.where(lane == row + shift, spread_stats, 0.0), axis=1, keepdims=True
    )


def layer_kernel(
    context_far, query_far, gain_far, w_query_far, w_key_far, value_far, lengths, block_out, query_out,
    context_rows, query_acts, gain, w_query, w_key, value_weight, load_sem,
    twin_query, twin_key, twin_value, sliced, query_sliced, gathered, partial, first_sum, passed,
    second_sum, query_sums, query_arrived, query_mine, query_parts, context, query,
    anchor, partials, own_partials, received, merged, merged_all,
    twin_send, twin_recv, row_send, row_recv, first_send, first_recv, passed_send, passed_recv,
    second_send, second_recv, query_send, query_recv, spread_send, spread_recv,
    scatter_send, column_send, plane_send, anchor_recv,
    partial_send, partial_recv, merged_send, merged_recv,
):
    outer, inner = lax.axis_index("outer"), lax.axis_index("inner")
    outers, inners = lax.axis_size("outer"), lax.axis_size("inner")
    devices = outers * inners
    me = outer * inners + inner
    loads = [
        pltpu.make_async_copy(far, near, load_sem.at[k])
        for k, (far, near) in enumerate(
            (
                (gain_far, gain), (context_far, context_rows), (w_key_far, w_key),
                (value_far, value_weight), (w_query_far, w_query), (query_far, query_acts),
            )
        )
    ]
    for load in loads:
        load.start()
    chip, core = inner // 2, inner % 2
    twin = chip * 2 + 1 - core

    def peer(step):
        return chip_peer(chip, step)

    def remote(source, target, send, recv, to_outer, to_inner):
        return pltpu.make_async_remote_copy(
            src_ref=source, dst_ref=target, send_sem=send, recv_sem=recv,
            device_id={"outer": to_outer, "inner": to_inner},
            device_id_type=pl.DeviceIdType.MESH,
        )

    barrier = pltpu.get_barrier_semaphore()

    def greet(t, carry):
        other = (me + t) % devices
        pl.semaphore_signal(
            barrier, inc=1, device_id={"outer": other // inners, "inner": other % inners},
            device_id_type=pl.DeviceIdType.MESH,
        )
        return carry

    lax.fori_loop(1, devices, greet, 0)
    loads[0].wait()
    loads[1].wait()

    @pl.loop(0, context_rows.shape[0] // 16)
    def _(index):
        first = pl.multiple_of(index * 16, 16)
        rows = normalize_rows(context_rows, gain, first, 16)
        for k in range(4):
            sliced[k, pl.ds(first, 16), :] = rows[:, k * 1024 : (k + 1) * 1024]

    pl.semaphore_wait(barrier, devices - 1)

    row_copies = [
        remote(
            sliced.at[peer(step)], gathered.at[step], row_send.at[step], row_recv.at[step],
            outer, peer(step) * 2 + core,
        )
        for step in range(3)
    ]
    for step in (2, 0, 1):
        row_copies[step].start()

    for load in loads[2:]:
        load.wait()
    weight_copies = [
        remote(mine, theirs, twin_send.at[k], twin_recv.at[k], outer, twin)
        for k, (mine, theirs) in enumerate(
            ((w_key, twin_key), (value_weight, twin_value), (w_query, twin_query))
        )
    ]
    for copy in weight_copies:
        copy.start()

    @pl.loop(0, query_acts.shape[0] // 16)
    def _(index):
        first = pl.multiple_of(index * 16, 16)
        rows = normalize_rows(query_acts, gain, first, 16)
        for k in range(4):
            query_sliced[k, pl.ds(first, 16), :] = rows[:, k * 1024 : (k + 1) * 1024]

    gathered[3] = sliced[chip]
    for copy in weight_copies:
        copy.wait()

    def tiles(k):
        if k < 2:
            return (w_key, value_weight)[k][...], (twin_key, twin_value)[k][...]
        columns = slice((k - 2) * 512, (k - 1) * 512)
        return w_query[:, columns], twin_query[:, columns]

    own_columns = pl.ds(pl.multiple_of(core * 512, 512), 512)
    twin_columns = pl.ds(pl.multiple_of((1 - core) * 512, 512), 512)

    def product(source, index, k):
        own_tile, twin_tile = tiles(k)
        return jnp.dot(
            source[index, :, own_columns], own_tile, preferred_element_type=jnp.float32
        ) + jnp.dot(
            source[index, :, twin_columns], twin_tile, preferred_element_type=jnp.float32
        )

    for k in range(6):
        query_sums[:, k * 512 : (k + 1) * 512] = product(query_sliced, chip, k)

    def query_part(other):
        return pl.ds(pl.multiple_of(other * 16 + core * 8, 8), 8)

    query_copies = [
        remote(
            query_sums.at[query_part(peer(step))], query_arrived.at[step], query_send.at[step],
            query_recv.at[step], outer, peer(step) * 2 + core,
        )
        for step in range(3)
    ]
    for copy in query_copies:
        copy.start()

    def first_copy(k):
        return remote(
            partial.at[k % 2, k], first_sum.at[k], first_send.at[k], first_recv.at[k],
            outer, peer(k % 2) * 2 + core,
        )

    def passed_copy(k):
        return remote(
            partial.at[2, k], passed.at[k], passed_send.at[k], passed_recv.at[k],
            outer, peer(k % 2) * 2 + core,
        )

    def second_copy(k):
        return remote(
            partial.at[1 - k % 2, k], second_sum.at[k], second_send.at[k], second_recv.at[k],
            outer, peer(1 - k % 2) * 2 + core,
        )

    def multiply(k):
        def one(step, carry):
            partial[step, k] = product(gathered, step, k)
            return carry

        lax.fori_loop(0, 4, one, 0)
        passed_copy(k).start()
        first_copy(k).start()

    def relay(k):
        passed_copy(k).wait()
        partial[1 - k % 2, k] = partial[1 - k % 2, k] + passed[k]
        second_copy(k).start()

    def settle(k):
        first_copy(k).wait()
        second_copy(k).wait()
        total = partial[3, k] + first_sum[k] + second_sum[k]
        context[:, k * 512 : (k + 1) * 512] = total.astype(jnp.bfloat16)

    row_copies[2].wait()
    for k in range(2):
        partial[2, k] = product(gathered, 2, k)
        passed_copy(k).start()
    for step in range(2):
        row_copies[step].wait()
    for k in range(2):
        partial[k % 2, k] = product(gathered, k % 2, k)
        first_copy(k).start()
    for k in range(2, 4):
        multiply(k)
    for k in range(2):
        partial[1 - k % 2, k] = product(gathered, 1 - k % 2, k)
        partial[3, k] = product(gathered, 3, k)

    for copy in query_copies:
        copy.wait()
    query_mine[...] = (
        query_sums[query_part(chip), :] + query_arrived[0] + query_arrived[1] + query_arrived[2]
    ).astype(jnp.bfloat16).astype(jnp.float32)

    spread_copies = [
        remote(
            query_mine, query_parts.at[core, chip], spread_send.at[step], spread_recv.at[step],
            outer, peer(step) * 2 + core,
        )
        for step in range(3)
    ]
    for copy in spread_copies:
        copy.start()
    query_parts[core, chip] = query_mine[...]
    relay(0)
    relay(1)
    for k in range(4, 6):
        multiply(k)

    for copy in spread_copies:
        copy.wait()
    twin_copy = remote(
        query_parts.at[core], query_parts.at[core], spread_send.at[3], spread_recv.at[3],
        outer, twin,
    )
    twin_copy.start()
    relay(2)
    relay(3)
    twin_copy.wait()
    for pair in range(4):
        query[pair * 16 : (pair + 1) * 16] = jnp.concatenate(
            [query_parts[0, pair], query_parts[1, pair]], axis=0
        ).astype(jnp.bfloat16)
    settle(0)
    settle(1)

    def scatter_copy(j):
        return remote(
            context.at[:, pl.ds(j * 128, 128)], anchor.at[j], scatter_send.at[j],
            anchor_recv.at[j], 0, j,
        )

    @pl.when(me == 0)
    def _():
        for j in range(1, 8):
            scatter_copy(j).start()
        anchor[0] = context[:, 0:128]

    own_length, anchor_length = lengths[me], lengths[0]

    for h in range(4):
        keys = context[:, h * 128 : (h + 1) * 128]
        values = context[:, 512 + h * 128 : 512 + (h + 1) * 128]
        reached = iota((256, 128), 1) < own_length
        store_partials(partials, h, masked_softmax(head_rows(query, h), keys, values, reached))

    def partial_copy(other):
        return lambda slot: remote(
            partials.at[other], received.at[slot], partial_send.at[other], partial_recv.at[slot],
            other // inners, other % inners,
        )

    def send_partial(t, carry):
        partial_copy((me + t) % devices)(me).start()
        return carry

    lax.fori_loop(1, devices, send_partial, 0)

    relay(4)
    relay(5)

    def column_copy(o):
        return remote(
            anchor.at[inner], anchor.at[inner], column_send.at[o], anchor_recv.at[inner], o, inner
        )

    def plane_copy(j, slot):
        return remote(
            anchor.at[slot], anchor.at[slot], plane_send.at[j], anchor_recv.at[slot], outer, j
        )

    @pl.when(me != 0)
    def _():
        plane_copy(inner, inner).wait_recv()

    @pl.when(outer == 0)
    def _():
        for o in range(1, 4):
            column_copy(o).start()

    def send_plane(t, carry):
        plane_copy((inner + t) % inners, inner).start()
        return carry

    lax.fori_loop(1, inners, send_plane, 0)

    for h in range(4):
        keys = query[:, h * 128 : (h + 1) * 128]
        values = query[:, 512 + h * 128 : 512 + (h + 1) * 128]
        causal = iota((256, 64), 0) % 64 >= iota((256, 64), 1)
        store_partials(own_partials, h, masked_softmax(head_rows(query, h), keys, values, causal))
    received[me] = partials[me]
    received[devices] = own_partials[me]

    def wait_partial(t, carry):
        other = (me + t) % devices
        partial_copy(other)(other).wait()
        return carry

    lax.fori_loop(1, devices, wait_partial, 0)

    def highest(s, peak):
        return jnp.maximum(peak, stat_column(received[s, 32:33], 0))

    top = lax.fori_loop(
        0, devices + 1, highest, jnp.full((32, 1), -jnp.inf, jnp.float32)
    )

    def add_up(s, carry):
        total, numerator = carry
        factor = jnp.exp(stat_column(received[s, 32:33], 0) - top)
        return (
            total + stat_column(received[s, 32:33], 32) * factor,
            numerator + received[s, 0:32] * factor,
        )

    total, numerator = lax.fori_loop(
        0, devices + 1, add_up,
        (jnp.zeros((32, 1), jnp.float32), jnp.zeros((32, 128), jnp.float32)),
    )
    merged[...] = (numerator / total).astype(jnp.bfloat16)

    def merged_copy(other, slot):
        return remote(
            merged, merged_all.at[slot], merged_send.at[other], merged_recv.at[slot],
            other // inners, other % inners,
        )

    def send_merged(t, carry):
        merged_copy((me + t) % devices, me).start()
        return carry

    lax.fori_loop(1, devices, send_merged, 0)
    merged_all[me] = merged[...]

    def wait_plane(t, carry):
        other = (inner + t) % inners
        plane_copy(other, inner).wait_send()
        plane_copy(other, other).wait_recv()
        return carry

    lax.fori_loop(1, inners, wait_plane, 0)

    row, column = iota((512, 256), 0) % 128, iota((512, 256), 1)
    place = column % 128
    limit = jnp.where(column < 128, jnp.where(me > 0, anchor_length, 0), own_length)
    allowed = (place < limit) & ((column < 128) | (row >= place))
    for h in range(4):
        settle(2 + h)
        keys = jnp.concatenate([anchor[h], context[:, h * 128 : (h + 1) * 128]], axis=0)
        values = jnp.concatenate(
            [anchor[4 + h], context[:, 512 + h * 128 : 512 + (h + 1) * 128]], axis=0
        )
        _, sum_exp, numerator = masked_softmax(head_rows(context, h), keys, values, allowed)
        result = (numerator / sum_exp).astype(jnp.bfloat16)
        for g in range(4):
            block_out[:, (h * 4 + g) * 128 : (h * 4 + g + 1) * 128] = result[
                g * 128 : (g + 1) * 128
            ]

    @pl.when(me == 0)
    def _():
        for j in range(1, 8):
            scatter_copy(j).wait_send()

    @pl.when(outer == 0)
    def _():
        for o in range(1, 4):
            column_copy(o).wait_send()

    def wait_merged(t, carry):
        other = (me + t) % devices
        merged_copy(other, other).wait()
        return carry

    lax.fori_loop(1, devices, wait_merged, 0)
    for d in range(32):
        query_out[d % 2 * 32 : d % 2 * 32 + 32, d // 2 * 128 : d // 2 * 128 + 128] = merged_all[d]


def layer(context, query_acts, norm_gain, w_query, w_key, value_weight, lengths):
    vmem = pl.BlockSpec(memory_space=pltpu.VMEM)
    bf16, f32, dma = jnp.bfloat16, jnp.float32, pltpu.SemaphoreType.DMA
    buffers = [
        ((512, 2048), bf16), ((512, 512), bf16), ((512, 512), bf16),
        ((4, 128, 1024), bf16), ((4, 64, 1024), bf16), ((4, 128, 1024), bf16),
        ((4, 6, 128, 512), f32), ((6, 128, 512), f32), ((6, 128, 512), f32),
        ((6, 128, 512), f32), ((64, 3072), f32), ((3, 8, 3072), f32), ((8, 3072), f32),
        ((2, 4, 8, 3072), f32), ((128, 3072), bf16), ((64, 3072), bf16),
        ((8, 128, 128), bf16), ((32, 40, 128), f32), ((32, 40, 128), f32),
        ((33, 40, 128), f32), ((32, 128), bf16), ((32, 32, 128), bf16),
    ]
    counts = [3, 3, 3, 3, 6, 6, 6, 6, 6, 6, 3, 3, 8, 8, 8, 4, 8, 8, 32, 32, 32, 32]
    return pl.pallas_call(
        layer_kernel,
        out_shape=[
            jax.ShapeDtypeStruct((128, 2048), bf16),
            jax.ShapeDtypeStruct((64, 2048), bf16),
        ],
        in_specs=[pl.BlockSpec(memory_space=pltpu.HBM)] * 6
        + [pl.BlockSpec(memory_space=pltpu.SMEM)],
        out_specs=[vmem] * 2,
        scratch_shapes=[
            pltpu.VMEM((128, 4096), bf16), pltpu.VMEM((64, 4096), bf16), pltpu.VMEM((1, 4096), f32),
            pltpu.VMEM((512, 2048), bf16), pltpu.VMEM((512, 512), bf16),
            pltpu.VMEM((512, 512), bf16), dma((6,)),
        ]
        + [pltpu.VMEM(shape, kind) for shape, kind in buffers]
        + [dma((count,)) for count in counts],
        compiler_params=pltpu.CompilerParams(
            collective_id=0, has_side_effects=True, vmem_limit_bytes=56 * 2**20
        ),
        cost_estimate=pl.CostEstimate(
            flops=5 * 10**9, bytes_accessed=8 * 2**20, transcendentals=10**6
        ),
    )(context, query_acts, norm_gain.reshape(1, -1), w_query, w_key, value_weight, lengths)


def attend_part(query_rows, key_row_block, value_matrix, allowed):
    count_of_rows = query_rows.shape[0]
    head_groups = query_rows.reshape(
        count_of_rows, KEY_VALUE_HEADS, QUERY_HEADS // KEY_VALUE_HEADS, HEAD_SIZE
    )
    per_head_keys = key_row_block.reshape(key_row_block.shape[0], KEY_VALUE_HEADS, HEAD_SIZE)
    per_head_values = value_matrix.reshape(value_matrix.shape[0], KEY_VALUE_HEADS, HEAD_SIZE)
    scores = jnp.einsum(
        "rhgd,khd->hgrk", head_groups, per_head_keys, preferred_element_type=jnp.float32
    ) * HEAD_SIZE ** (-0.5)
    scores = jnp.where(allowed, scores, -jnp.inf)
    maxima = jnp.max(scores, axis=-1)
    weights = jnp.exp(scores - maxima[..., None])
    sum_exp = jnp.sum(weights, axis=-1)
    numerator = jnp.einsum(
        "hgrk,khd->rhgd",
        weights.astype(jnp.bfloat16),
        per_head_values,
        preferred_element_type=jnp.float32,
    )
    return (
        maxima.reshape(QUERY_HEADS, count_of_rows),
        sum_exp.reshape(QUERY_HEADS, count_of_rows),
        numerator.reshape(count_of_rows, QUERY_HEADS * HEAD_SIZE),
    )


def spread(factor):
    return jnp.repeat(factor.T, HEAD_SIZE, axis=1)


def combine(former, latter):
    maxima = jnp.maximum(former[0], latter[0])
    scale_one = jnp.exp(former[0] - maxima)
    scale_two = jnp.exp(latter[0] - maxima)
    return (
        maxima,
        former[1] * scale_one + latter[1] * scale_two,
        former[2] * spread(scale_one) + latter[2] * spread(scale_two),
    )


def finish(pieces):
    return (pieces[2] / spread(pieces[1])).astype(jnp.bfloat16)


def share_anchor(stacked):
    return broadcast(stacked, ("outer", "inner"), 0)


def project_all(context, query_acts, norm_gain, w_query, w_key, value_weight):
    normed = jnp.concatenate(
        [normalize(context, norm_gain), normalize(query_acts, norm_gain)], axis=0
    )
    return tuple(
        jnp.dot(
            normed,
            lax.all_gather(weight, "inner", axis=0, tiled=True),
            preferred_element_type=jnp.float32,
        ).astype(jnp.bfloat16)
        for weight in (w_query, w_key, value_weight)
    )


def per_device(context, query_acts, norm_gain, w_query, w_key, value_weight, lengths):
    if (lax.axis_size("outer"), lax.axis_size("inner")) == (4, 8):
        return tuple(
            layer(context, query_acts, norm_gain, w_query, w_key, value_weight, lengths)
        )
    block_rows = context.shape[0]
    projected_q, projected_k, projected_v = project_all(
        context, query_acts, norm_gain, w_query, w_key, value_weight
    )
    anchor = share_anchor(jnp.stack([projected_k[:block_rows], projected_v[:block_rows]]))
    position = lax.axis_index(("outer", "inner"))
    own_length = lengths[position]
    anchor_length = lengths[0]
    places = jnp.arange(block_rows, dtype=jnp.int32)
    causal = places[:, None] >= places[None, :]
    block_q = projected_q[:block_rows]
    block_k = projected_k[:block_rows]
    block_v = projected_v[:block_rows]
    query_q = projected_q[block_rows:]
    query_k = projected_k[block_rows:]
    query_v = projected_v[block_rows:]
    query_count = query_q.shape[0]
    own_allowed = causal & (places[None, :] < own_length)
    anchor_allowed = jnp.broadcast_to(
        (places[None, :] < anchor_length) & (position > 0), (block_rows, block_rows)
    )
    allowed = jnp.concatenate([anchor_allowed, own_allowed], axis=1)
    key_row_block = jnp.concatenate([anchor[0], block_k], axis=0)
    value_rows = jnp.concatenate([anchor[1], block_v], axis=0)
    block_out = finish(attend_part(block_q, key_row_block, value_rows, allowed))
    reached = jnp.broadcast_to(places[None, :] < own_length, (query_count, block_rows))
    block_part = attend_part(query_q, block_k, block_v, reached)
    highest = lax.pmax(block_part[0], ("outer", "inner"))
    rescale = jnp.exp(block_part[0] - highest)
    summed_parts = lax.psum(
        (block_part[1] * rescale, block_part[2] * spread(rescale)), ("outer", "inner")
    )
    merged = (highest, summed_parts[0], summed_parts[1])
    query_places = jnp.arange(query_count, dtype=jnp.int32)
    self_part = attend_part(
        query_q, query_k, query_v, query_places[:, None] >= query_places[None, :]
    )
    return (block_out, finish(combine(merged, self_part)))


def solution(mesh):
    in_specs = (
        P(("outer", "inner"), None),
        P(),
        P(),
        P("inner", None),
        P("inner", None),
        P("inner", None),
        P(),
    )
    out_specs = (P(("outer", "inner"), None), P())
    return jax.shard_map(
        per_device, mesh=mesh, in_specs=in_specs, out_specs=out_specs, check_vma=False
    )
```
